32 devices in a mesh: groups: 2 (over y), img: 4 (over z), pair: 4 (over x, core).
Axes of the slice: x: 2, y: 2, z: 4, core: 2. Of those that a mesh axis runs over, the one named last changes fastest.
Arguments:
- pair_images: int32 [128, 2], P(('groups', 'img')), parts along dimension 0, may hold values from 0 to 31, as said below
- pointmaps: bfloat16 [128, 2, 3, 50176], P(('groups', 'img'), None, None, 'pair'), parts along dimension 0, may hold values from -6 to 6
- confidence: bfloat16 [128, 2, 50176], P(('groups', 'img'), None, 'pair'), parts along dimension 0, may hold values from 1 to 10
- log_depth: float32 [64, 50176], P(('groups', 'img'), 'pair'), parts along dimension 0, may hold values from -0.5 to 0.5
- image_params: float32 [64, 7], P(('groups', 'img')), parts along dimension 0, may hold values from -0.3 to 0.3
- pair_params: float32 [128, 7], P(('groups', 'img')), parts along dimension 0, may hold values from -0.3 to 0.3
Outputs:
- new_depth: float32 [64, 50176], P(('groups', 'img'), 'pair'), parts along dimension 0
- new_images: float32 [64, 7], P(('groups', 'img')), parts along dimension 0
- new_pairs: float32 [128, 7], P(('groups', 'img')), parts along dimension 0
The draws below stay inside these ranges and needn't reach their ends.
There are 2 independent parts, one for each index of `groups`. The reference program is written for one: setup_inputs(seed, part) draws one part's arguments, and reference() takes and returns one part's arrays. A program takes and returns all parts, laid end to end along the dimension named above; each array names one. Nothing has to cross between parts.
Inputs may be any that keep to these rules, and one draw needn't show every extreme that they name: pair_images[e, 0] is one of the 8 images of block e // 16, i.e. between (e // 16) * 8 and that plus 8 - 1; the two images of a pair differ; within each aligned block of 16 pairs at most 8 second images lie in any one aligned block of 8 images, and exactly 8 in some block.
All inputs are finite; a program needn't handle non-finite values.
Results may differ from the reference program's by a relative error of at most 0.0003.
Values may be sent and summed in bfloat16 or wider, within the bound.
A program may use at most 128 MiB of HBM per device.

```python
import math
import jax
import jax.numpy as jnp
from jax import lax

SIDE = 224
PIX = 50176
IMG_DEV = 8
PAIR_DEV = 16
STEPS = 3
IMAGES = 32
PAIRS = 64
CAP = 8


def draw_pair_images(key, part):
    key = jax.random.fold_in(key, 11)
    blocks = PAIRS // PAIR_DEV
    keys = jax.random.split(key, blocks)

    def one_block(block_key, block):
        parts = jax.random.split(block_key, 6)
        busiest = jax.random.randint(parts[0], (), 0, blocks)
        scores = jax.random.permutation(parts[1], blocks * CAP)
        slot_block = jnp.arange(blocks * CAP) // CAP
        scores = scores - jnp.where(slot_block == busiest, blocks * CAP, 0)
        chosen = jnp.argsort(scores)[:PAIR_DEV]
        chosen = jax.random.permutation(parts[2], chosen)
        target = chosen // CAP
        first_in = jax.random.randint(parts[3], (PAIR_DEV,), 0, IMG_DEV)
        other_in = jax.random.randint(parts[4], (PAIR_DEV,), 0, IMG_DEV)
        moved_in = (first_in + 1 + jax.random.randint(parts[5], (PAIR_DEV,), 0, IMG_DEV - 1)) % IMG_DEV
        second_in = jnp.where(target == block, moved_in, other_in)
        return jnp.stack([block * IMG_DEV + first_in, target * IMG_DEV + second_in], 1)
    result = jax.vmap(one_block)(keys, jnp.arange(blocks))
    return result.reshape(PAIRS, 2).astype(jnp.int32)


def level_of(own_key, extent, cuts, least, largest):
    factor_of = 1.0
    for dim, shards_of in cuts:
        heights = jax.random.uniform(jax.random.fold_in(jax.random.fold_in(own_key, 6), dim), (shards_of,), jnp.float32, least / len(cuts), largest / len(cuts))
        factor_of = factor_of * jnp.repeat(jnp.exp(heights), extent[dim] // shards_of).reshape((-1,) + (1,) * (len(extent) - 1 - dim))
    return factor_of


def scatter_about(key, extent, scale, reach, cuts=(), held_as=jnp.bfloat16):
    loudness = level_of(key, extent, cuts, -0.22, 0.18) if cuts else 1.0
    values = jax.random.normal(key, extent, jnp.float32) * scale * loudness
    return jnp.minimum(jnp.maximum(values, -reach), reach).astype(held_as)


def setup_inputs(seed: int = 0, part: int = 0) -> dict:
    seeds = jax.random.split(jax.random.key(seed), 7)
    own_keys = jax.random.split(jax.random.fold_in(seeds[6], part), 7)
    return {
        "pair_images": draw_pair_images(jax.random.fold_in(jax.random.fold_in(seeds[6], part), 71), part),
        "pointmaps": scatter_about(own_keys[1], (PAIRS, 2, 3, PIX), 1.0, 6.0, ((0, 4), (3, 4))),
        "confidence": jnp.clip(jnp.exp(math.log(10.0) - 2.3025851 * jax.random.uniform(own_keys[2], (PAIRS, 2, PIX), jnp.float32) ** level_of(own_keys[2], (PAIRS, 2, PIX), ((0, 4), (2, 4)), -0.2, 0.2)), 1.0, 10.0).astype(jnp.bfloat16),
        "log_depth": jnp.clip(jax.random.uniform(own_keys[3], (IMAGES, PIX), jnp.float32, -0.5, 0.5) * level_of(own_keys[3], (IMAGES, PIX), ((0, 4), (1, 4)), -0.4, 0.0), -0.5, 0.5),
        "image_params": jnp.clip(jax.random.uniform(own_keys[4], (IMAGES, 7), jnp.float32, -0.3, 0.3) * level_of(own_keys[4], (IMAGES, 7), ((0, 4),), -0.4, 0.0), -0.3, 0.3),
        "pair_params": jnp.clip(jax.random.uniform(own_keys[5], (PAIRS, 7), jnp.float32, -0.3, 0.3) * level_of(own_keys[5], (PAIRS, 7), ((0, 4),), -0.4, 0.0), -0.3, 0.3),
    }


def rotate(w, v):
    scale = 2.0 / (1.0 + w[0] * w[0] + w[1] * w[1] + w[2] * w[2])
    c0 = w[1] * v[2] - w[2] * v[1]
    c1 = w[2] * v[0] - w[0] * v[2]
    c2 = w[0] * v[1] - w[1] * v[0]
    e0 = w[1] * c2 - w[2] * c1
    e1 = w[2] * c0 - w[0] * c2
    e2 = w[0] * c1 - w[1] * c0
    return jnp.stack([v[0] + scale * (c0 + e0), v[1] + scale * (c1 + e1), v[2] + scale * (c2 + e2)])

def view_grads(depth, image, pose, maps, conf, coord_a, coord_b):
    points = maps.astype(jnp.float32)
    weight = conf.astype(jnp.float32)

    def loss(zz, ii, qq):
        focal = jnp.exp(ii[0])
        dist = jnp.exp(zz)
        camera = jnp.stack([dist * coord_a / focal, dist * coord_b / focal, dist])
        world = rotate(ii[1:4], camera) + ii[4:7][:, None]
        aligned = jnp.exp(qq[0]) * rotate(qq[1:4], points) + qq[4:7][:, None]
        resid = world - aligned
        return jnp.sum(weight * lax.optimization_barrier(jnp.sum(resid * resid, 0)))
    value, pull = jax.vjp(loss, depth, image, pose)
    d_depth, d_image, d_pose = pull(jnp.ones_like(value))
    focal = jnp.exp(image[0])
    dist = jnp.exp(depth)
    curv = 2.0 * weight * dist * dist * ((coord_a * coord_a + coord_b * coord_b) / (focal * focal) + 1.0)
    return (d_depth, d_image, d_pose, curv, jnp.sum(weight))

def reference(pair_images, pointmaps, confidence, log_depth, image_params, pair_params):
    pixel = jnp.arange(PIX)
    coord_a = ((pixel % SIDE).astype(jnp.float32) - (SIDE - 1) / 2.0) / SIDE
    coord_b = ((pixel // SIDE).astype(jnp.float32) - (SIDE - 1) / 2.0) / SIDE
    rate_img = jnp.array([0.1, 0.02, 0.02, 0.02, 0.3, 0.3, 0.3], jnp.float32)
    rate_pair = jnp.array([0.05, 0.02, 0.02, 0.02, 0.3, 0.3, 0.3], jnp.float32)
    for step in range(STEPS):

        def per_pair(carry, items):
            grad_z, curv_z, grad_i, weight_i = carry
            pair_ids, maps, conf, pose = items
            grad_p = jnp.zeros((7,), jnp.float32)
            weight_p = jnp.zeros((), jnp.float32)
            for view in range(2):
                image_id = pair_ids[view]
                d_z, d_i, d_p, curv, wsum = view_grads(log_depth[image_id], image_params[image_id], pose, maps[view], conf[view], coord_a, coord_b)
                grad_z = grad_z.at[image_id].add(d_z)
                curv_z = curv_z.at[image_id].add(curv)
                grad_i = grad_i.at[image_id].add(d_i)
                weight_i = weight_i.at[image_id].add(wsum)
                grad_p = grad_p + d_p
                weight_p = weight_p + wsum
            return ((grad_z, curv_z, grad_i, weight_i), (grad_p, weight_p))
        start = (jnp.zeros_like(log_depth), jnp.zeros_like(log_depth), jnp.zeros_like(image_params), jnp.zeros((IMAGES,), jnp.float32))
        (grad_z, curv_z, grad_i, weight_i), (grad_p, weight_p) = lax.scan(per_pair, start, (pair_images, pointmaps, confidence, pair_params))
        log_depth = log_depth - grad_z / (curv_z + 1.0)
        image_params = image_params - rate_img[None, :] * grad_i / (weight_i[:, None] + 1.0)
        pair_params = pair_params - rate_pair[None, :] * grad_p / (weight_p[:, None] + 1.0)
    return (log_depth, image_params, pair_params)
```

```python
import functools

import jax
import jax.numpy as jnp
from jax import lax
from jax.experimental import pallas as pl
from jax.experimental.pallas import tpu as pltpu
from jax.sharding import PartitionSpec as P

SIDE = 224
STEPS = 3
LANES = 128
CHUNK = 16
MESH = pl.DeviceIdType.MESH
ROWS = 40
SYM = ((0, 0), (0, 1), (0, 2), (1, 1), (1, 2), (2, 2))


def rot_rows(w):
    norm = w[0] * w[0] + w[1] * w[1] + w[2] * w[2]
    k = 2.0 / (1.0 + norm)
    cross = [[None, -w[2], w[1]], [w[2], None, -w[0]], [-w[1], w[0], None]]
    out = []
    for i in range(3):
        line = []
        for j in range(3):
            if i == j:
                line.append(1.0 + k * (w[i] * w[i] - norm))
            else:
                line.append(k * (cross[i][j] + w[i] * w[j]))
        out.append(line)
    return out


def rot_grad_rows(w, g):
    norm = w[0] * w[0] + w[1] * w[1] + w[2] * w[2]
    k = 2.0 / (1.0 + norm)
    trace = g[0][0] + g[1][1] + g[2][2]
    skew = [g[2][1] - g[1][2], g[0][2] - g[2][0], g[1][0] - g[0][1]]
    lin = [sum(g[i][j] * w[j] for j in range(3)) for i in range(3)]
    both = [lin[i] + sum(g[j][i] * w[j] for j in range(3)) for i in range(3)]
    value = sum(w[i] * (skew[i] + lin[i]) for i in range(3)) - norm * trace
    return [
        k * (skew[i] + both[i] - 2.0 * w[i] * trace) - k * k * w[i] * value for i in range(3)
    ]


def coef_rows(st):
    factor = jnp.exp(st[0])
    re = rot_rows(st[1:4])
    rg = rot_rows(st[8:11])
    gap = [st[4 + i] - st[11 + i] for i in range(3)]
    rows = []
    for j in range(3):
        for k in range(3):
            rows.append(factor * sum(rg[i][j] * re[i][k] for i in range(3)))
    for j in range(3):
        rows.append(sum(rg[i][j] * gap[i] for i in range(3)))
    rows.append(jnp.exp(-st[7]))
    zero = jnp.zeros_like(rows[0])
    return rows + [zero] * 3


def update_rows(st, mom, same, swap):
    factor = jnp.exp(st[0])
    u, w = st[1:4], st[8:11]
    re, rg = rot_rows(u), rot_rows(w)
    gap = [st[11 + i] - st[4 + i] for i in range(3)]
    d1 = mom[0:3]
    tx = [mom[3 + 3 * j : 6 + 3 * j] for j in range(3)]
    s0 = mom[16]
    s1 = mom[17:20]
    s2, dd = {}, {}
    for n, (i, j) in enumerate(SYM):
        s2[i, j] = s2[j, i] = mom[20 + n]
        dd[i, j] = dd[j, i] = mom[32 + n]
    sre = [[factor * re[i][j] for j in range(3)] for i in range(3)]

    def dot(left, right):
        return left[0] * right[0] + left[1] * right[1] + left[2] * right[2]

    shift = [2.0 * (dot(rg[i], d1) + gap[i] * s0 - dot(sre[i], s1)) for i in range(3)]
    mx = [
        [
            2.0
            * (
                dot(rg[i], [tx[j][k] for j in range(3)])
                + gap[i] * s1[k]
                - dot(sre[i], [s2[j, k] for j in range(3)])
            )
            for k in range(3)
        ]
        for i in range(3)
    ]
    mc = [
        [
            2.0
            * (
                dot(rg[i], [dd[j, k] for j in range(3)])
                + gap[i] * d1[k]
                - dot(sre[i], tx[k])
            )
            for k in range(3)
        ]
        for i in range(3)
    ]
    d_scale = -sum(mx[i][k] * sre[i][k] for i in range(3) for k in range(3))
    d_spin = rot_grad_rows(u, [[-factor * mx[i][k] for k in range(3)] for i in range(3)])
    d_turn = rot_grad_rows(w, mc)
    d_focal = -sum(rg[i][j] * mc[i][j] for i in range(3) for j in range(2))
    grads_p = jnp.concatenate([d_scale] + d_spin + [-x for x in shift] + [s0], 0)
    grads_i = jnp.concatenate([d_focal] + d_turn + shift + [s0], 0)
    grads_p = grads_p + swap(grads_p)
    grads_i = jnp.dot(
        grads_i,
        same,
        precision=lax.Precision.HIGHEST,
        preferred_element_type=jnp.float32,
    )
    rate_p = (0.05, 0.02, 0.02, 0.02, 0.3, 0.3, 0.3)
    rate_i = (0.1, 0.02, 0.02, 0.02, 0.3, 0.3, 0.3)
    down_p = 1.0 / (grads_p[7:8] + 1.0)
    down_i = 1.0 / (grads_i[7:8] + 1.0)
    new = [st[i] - rate_p[i] * grads_p[i : i + 1] * down_p for i in range(7)]
    new += [st[7 + i] - rate_i[i] * grads_i[i : i + 1] * down_i for i in range(7)]
    return new


def step_kernel(first, meta, rep, coef, own, far, z_ref, a_ref, b_ref, *rest):
    if first:
        z_out, mom_out, dc, total, weights = rest
    else:
        before, z_out, mom_out, dc, total, weights = rest
    images, rows, _ = z_ref.shape
    views = coef.shape[1]
    own_count, far_count = own.shape[0], meta.shape[1] - own.shape[0]
    lane = lax.broadcasted_iota(jnp.int32, (1, views), 1)
    cuts = [pl.ds(c * CHUNK, CHUNK) for c in range(rows // CHUNK)]

    mom_out[...] = jnp.zeros_like(mom_out)
    if not first:
        mom_out[16:32, :] = before[16:32, :]

    def half(x):
        return x[0:8] + x[8:16]

    def put(row, sums, column):
        lines = [jnp.sum(x, 0, keepdims=True) for x in sums]
        count = -(-len(lines) // 8) * 8
        lines += [jnp.zeros_like(lines[0])] * (count - len(lines))
        value = jnp.sum(jnp.concatenate(lines, 0), 1, keepdims=True)
        mom_out[row : row + count, :] += jnp.where(lane == column, value, 0.0)

    def prepare(g, _):
        inv = coef[12, rep[g]]
        for cut in cuts:
            d = jnp.exp(z_ref[g, cut, :])
            near = d * inv
            dc[g, 0, cut, :] = near * a_ref[cut, :]
            dc[g, 1, cut, :] = near * b_ref[cut, :]
            dc[g, 2, cut, :] = d
            total[g, cut, :] = jnp.zeros((CHUNK, LANES), jnp.float32)
            weights[g, cut, :] = jnp.zeros((CHUNK, LANES), jnp.float32)
        return 0

    lax.fori_loop(0, images, prepare, 0)

    def view(data, slot, g, column):
        q = [[coef[3 * j + k, column] for k in range(3)] for j in range(3)]
        p = [coef[9 + j, column] for j in range(3)]
        sums = None
        consts = None
        for cut in cuts:
            x = [data[slot, k, cut, :].astype(jnp.float32) for k in range(3)]
            w = data[slot, 3, cut, :].astype(jnp.float32)
            y = [dc[g, j, cut, :] * w for j in range(3)]
            t = [[y[j] * x[k] for k in range(3)] for j in range(3)]
            pull = p[0] * y[0] + p[1] * y[1] + p[2] * y[2]
            for j in range(3):
                for k in range(3):
                    pull = pull + q[j][k] * t[j][k]
            total[g, cut, :] += pull
            weights[g, cut, :] += w
            new = [half(v) for v in y] + [half(t[j][k]) for j in range(3) for k in range(3)]
            sums = new if sums is None else [s + v for s, v in zip(sums, new)]
            if first:
                wx = [w * x[k] for k in range(3)]
                new = [half(w)] + [half(v) for v in wx]
                new += [half(wx[i] * x[j]) for i, j in SYM]
                consts = new if consts is None else [s + v for s, v in zip(consts, new)]
        put(0, sums, column)
        if first:
            put(16, consts, column)

    def own_view(i, _):
        view(own, meta[1, i], meta[2, i], meta[3, i])
        return 0

    lax.fori_loop(0, own_count, own_view, 0)

    def far_view(i, _):
        at = own_count + i

        @pl.when(meta[0, at] > 0)
        def _():
            view(far, meta[1, at], meta[2, at], meta[3, at])

        return 0

    lax.fori_loop(0, far_count, far_view, 0)

    def finish(g, _):
        sums = None
        for cut in cuts:
            c = [dc[g, j, cut, :] for j in range(3)]
            w = weights[g, cut, :]
            wc = [w * c[j] for j in range(3)]
            twice = 2.0 * (wc[0] * c[0] + wc[1] * c[1] + wc[2] * c[2])
            z_out[g, cut, :] = z_ref[g, cut, :] - (twice - 2.0 * total[g, cut, :]) / (twice + 1.0)
            new = [half(wc[i] * c[j]) for i, j in SYM]
            sums = new if sums is None else [s + v for s, v in zip(sums, new)]
        put(32, sums, rep[g])
        return 0

    lax.fori_loop(0, images, finish, 0)


def run_step(first, meta, rep, coef, own, far, z, a, b, before):
    images, rows, _ = z.shape
    views = coef.shape[1]
    smem = pl.BlockSpec(memory_space=pltpu.SMEM)
    vmem = pl.BlockSpec(memory_space=pltpu.VMEM)
    args = [meta, rep, coef, own, far, z, a, b] + ([] if first else [before])
    return pl.pallas_call(
        functools.partial(step_kernel, first),
        out_shape=(
            jax.ShapeDtypeStruct(z.shape, jnp.float32),
            jax.ShapeDtypeStruct((ROWS, views), jnp.float32),
        ),
        in_specs=[smem] * 3 + [vmem] * (len(args) - 3),
        out_specs=(vmem, vmem),
        scratch_shapes=[
            pltpu.VMEM((images, 3, rows, LANES), jnp.float32),
            pltpu.VMEM((images, rows, LANES), jnp.float32),
            pltpu.VMEM((images, rows, LANES), jnp.float32),
        ],
        compiler_params=pltpu.CompilerParams(vmem_limit_bytes=32 * 1024 * 1024),
    )(*args)


def share_kernel(
    n_pair, n_img, mom, state, same, state_out, coef_out, buf1, buf2, s1, r1, s2, r2
):
    views = mom.shape[1]
    stages = (("pair", n_pair, buf1, s1, r1), ("img", n_img, buf2, s2, r2))
    barrier = pltpu.get_barrier_semaphore()
    for axis, size, _, _, _ in stages:
        me = lax.axis_index(axis)
        for k in range(1, size):
            peer = lax.rem(me + k, size)
            pl.semaphore_signal(barrier, inc=1, device_id={axis: peer}, device_id_type=MESH)
    pl.semaphore_wait(barrier, n_pair + n_img - 2)

    value = mom[...]
    for axis, size, buf, send, recv in stages:
        me = lax.axis_index(axis)
        buf[me] = value
        copies = []
        for k in range(1, size):
            peer = lax.rem(me + k, size)
            copy = pltpu.make_async_remote_copy(
                src_ref=buf.at[me],
                dst_ref=buf.at[me],
                send_sem=send.at[k],
                recv_sem=recv.at[me],
                device_id={axis: peer},
                device_id_type=MESH,
            )
            copy.start()
            copies.append(copy)
        for k in range(1, size):
            peer = lax.rem(me + k, size)
            pltpu.make_async_remote_copy(
                src_ref=buf.at[peer],
                dst_ref=buf.at[peer],
                send_sem=send.at[k],
                recv_sem=recv.at[peer],
                device_id={axis: peer},
                device_id_type=MESH,
            ).wait_recv()
        value = buf[0]
        for k in range(1, size):
            value = value + buf[k]
        for copy in copies:
            copy.wait_send()

    moments = [value[i : i + 1] for i in range(ROWS)]
    st = [state[i : i + 1, :] for i in range(14)]
    new = update_rows(st, moments, same[...], lambda x: pltpu.roll(x, views // 2, axis=1))
    zero = jnp.zeros_like(new[0])
    state_out[...] = jnp.concatenate(new + [zero] * 2, 0)
    coef_out[...] = jnp.concatenate(coef_rows(new), 0)


def run_share(n_pair, n_img, mom, state, same):
    views = mom.shape[1]
    vmem = pl.BlockSpec(memory_space=pltpu.VMEM)
    return pl.pallas_call(
        functools.partial(share_kernel, n_pair, n_img),
        out_shape=(
            jax.ShapeDtypeStruct((16, views), jnp.float32),
            jax.ShapeDtypeStruct((16, views), jnp.float32),
        ),
        in_specs=[vmem] * 3,
        out_specs=(vmem, vmem),
        scratch_shapes=[
            pltpu.VMEM((n_pair, ROWS, views), jnp.float32),
            pltpu.VMEM((n_img, ROWS, views), jnp.float32),
            pltpu.SemaphoreType.DMA((n_pair,)),
            pltpu.SemaphoreType.DMA((n_pair,)),
            pltpu.SemaphoreType.DMA((n_img,)),
            pltpu.SemaphoreType.DMA((n_img,)),
        ],
        compiler_params=pltpu.CompilerParams(collective_id=0, has_side_effects=True),
    )(mom, state, same)


def per_device(pair_images, pointmaps, confidence, log_depth, image_params, pair_params):
    pair_dev = pair_images.shape[0]
    img_dev, pix_dev = log_depth.shape
    blocks = lax.axis_size("img")
    n_pair = lax.axis_size("pair")
    slots = max(2, 2 * pair_dev // blocks)
    here = lax.axis_index("img")
    rows = -(-pix_dev // (LANES * CHUNK)) * CHUNK
    pad = rows * LANES - pix_dev

    pixel = lax.axis_index("pair") * pix_dev + jnp.arange(rows * LANES)
    coord_a = ((pixel % SIDE).astype(jnp.float32) - (SIDE - 1) / 2.0) / SIDE
    coord_b = ((pixel // SIDE).astype(jnp.float32) - (SIDE - 1) / 2.0) / SIDE
    coord_a = coord_a.reshape(rows, LANES)
    coord_b = coord_b.reshape(rows, LANES)

    target = pair_images[:, 1] // img_dev
    hits = (target[:, None] == jnp.arange(blocks)[None, :]).astype(jnp.int32)
    rank = jnp.sum(jnp.cumsum(hits, 0) * hits, 1) - 1
    place = target * slots + rank
    source = jnp.sum(
        (place[None, :] == jnp.arange(blocks * slots)[:, None]) * jnp.arange(pair_dev)[None, :], 1
    )

    packed = jnp.concatenate([pointmaps, confidence[:, :, None, :]], 2)
    packed = jnp.pad(packed, ((0, 0), (0, 0), (0, 0), (0, pad)))
    packed = packed.reshape(pair_dev, 2, 4, rows, LANES)
    own = packed[:, 0]
    send = packed[:, 1][source].reshape(blocks, slots, 4, rows, LANES)
    far = lax.all_to_all(send, "img", split_axis=0, concat_axis=0, tiled=True)
    far = far.reshape(blocks * slots, 4, rows, LANES)

    small = jnp.concatenate(
        [
            pair_images.astype(jnp.float32).reshape(-1),
            pair_params.reshape(-1),
            image_params.reshape(-1),
        ]
    )
    small = lax.all_gather(small, "img")
    cut1, cut2 = 2 * pair_dev, 9 * pair_dev
    all_ids = small[:, :cut1].astype(jnp.int32).reshape(blocks * pair_dev, 2)
    all_pairs = small[:, cut1:cut2].reshape(blocks * pair_dev, 7)
    all_images = small[:, cut2:].reshape(blocks * img_dev, 7)
    image_of = all_ids.T.reshape(-1)
    views = image_of.shape[0]
    pairs = views // 2
    same = (image_of[:, None] == image_of[None, :]).astype(jnp.float32)
    hot = (image_of[None, :] == jnp.arange(blocks * img_dev)[:, None]).astype(jnp.float32)
    by_view = jnp.dot(
        all_images.T, hot, precision=lax.Precision.HIGHEST, preferred_element_type=jnp.float32
    )
    state = jnp.concatenate(
        [jnp.tile(all_pairs.T, (1, 2)), by_view, jnp.zeros((2, views), jnp.float32)], 0
    )
    coef = jnp.concatenate(coef_rows([state[i : i + 1] for i in range(14)]), 0)

    far_ids = all_ids[:, 1].reshape(blocks, pair_dev)
    mine = (far_ids // img_dev == here).astype(jnp.int32)
    far_slot = jnp.arange(blocks)[:, None] * slots + jnp.cumsum(mine, 1) - 1
    mine = mine.reshape(-1)
    meta = jnp.stack(
        [
            jnp.concatenate([jnp.ones((pair_dev,), jnp.int32), mine]),
            jnp.concatenate([jnp.arange(pair_dev), jnp.maximum(far_slot.reshape(-1), 0)]),
            jnp.concatenate([pair_images[:, 0] - here * img_dev, far_ids.reshape(-1) % img_dev]),
            jnp.concatenate([here * pair_dev + jnp.arange(pair_dev), pairs + jnp.arange(pairs)]),
        ]
    ).astype(jnp.int32)
    local = image_of[None, :] == here * img_dev + jnp.arange(img_dev)[:, None]
    rep = jnp.max(jnp.where(local, jnp.arange(views)[None, :], -1), 1)
    seen = rep >= 0
    rep = jnp.maximum(rep, 0).astype(jnp.int32)

    z = jnp.pad(log_depth, ((0, 0), (0, pad))).reshape(img_dev, rows, LANES)
    before = None
    for step in range(STEPS):
        z, mom = run_step(step == 0, meta, rep, coef, own, far, z, coord_a, coord_b, before)
        before = mom
        state, coef = run_share(n_pair, blocks, mom, state, same)

    new_depth = z.reshape(img_dev, rows * LANES)[:, :pix_dev]
    new_pairs = lax.dynamic_slice(state, (0, here * pair_dev), (7, pair_dev)).T
    new_images = jnp.where(seen[:, None], state[7:14][:, rep].T, image_params)
    return (new_depth, new_images, new_pairs)


def solution(mesh):
    in_specs = (
        P(("groups", "img"), None),
        P(("groups", "img"), None, None, "pair"),
        P(("groups", "img"), None, "pair"),
        P(("groups", "img"), "pair"),
        P(("groups", "img"), None),
        P(("groups", "img"), None),
    )
    out_specs = (
        P(("groups", "img"), "pair"),
        P(("groups", "img"), None),
        P(("groups", "img"), None),
    )
    return jax.shard_map(
        per_device, mesh=mesh, in_specs=in_specs, out_specs=out_specs, check_vma=False
    )
```

```python
import functools

import jax
import jax.numpy as jnp
from jax import lax
from jax.experimental import pallas as pl
from jax.experimental.pallas import tpu as pltpu
from jax.sharding import PartitionSpec as P

SIDE = 224
STEPS = 3
LANES = 128
CHUNK = 16
MESH = pl.DeviceIdType.MESH
ROWS = 40
SYM = ((0, 0), (0, 1), (0, 2), (1, 1), (1, 2), (2, 2))


def rot_rows(w):
    norm = w[0] * w[0] + w[1] * w[1] + w[2] * w[2]
    k = 2.0 / (1.0 + norm)
    cross = [[None, -w[2], w[1]], [w[2], None, -w[0]], [-w[1], w[0], None]]
    out = []
    for i in range(3):
        line = []
        for j in range(3):
            if i == j:
                line.append(1.0 + k * (w[i] * w[i] - norm))
            else:
                line.append(k * (cross[i][j] + w[i] * w[j]))
        out.append(line)
    return out


def rot_grad_rows(w, g):
    norm = w[0] * w[0] + w[1] * w[1] + w[2] * w[2]
    k = 2.0 / (1.0 + norm)
    trace = g[0][0] + g[1][1] + g[2][2]
    skew = [g[2][1] - g[1][2], g[0][2] - g[2][0], g[1][0] - g[0][1]]
    lin = [sum(g[i][j] * w[j] for j in range(3)) for i in range(3)]
    both = [lin[i] + sum(g[j][i] * w[j] for j in range(3)) for i in range(3)]
    value = sum(w[i] * (skew[i] + lin[i]) for i in range(3)) - norm * trace
    return [
        k * (skew[i] + both[i] - 2.0 * w[i] * trace) - k * k * w[i] * value for i in range(3)
    ]


def coef_rows(st):
    factor = jnp.exp(st[0])
    re = rot_rows(st[1:4])
    rg = rot_rows(st[8:11])
    gap = [st[4 + i] - st[11 + i] for i in range(3)]
    rows = []
    for j in range(3):
        for k in range(3):
            rows.append(factor * sum(rg[i][j] * re[i][k] for i in range(3)))
    for j in range(3):
        rows.append(sum(rg[i][j] * gap[i] for i in range(3)))
    rows.append(jnp.exp(-st[7]))
    zero = jnp.zeros_like(rows[0])
    return rows + [zero] * 3


def update_rows(st, mom, same, swap):
    factor = jnp.exp(st[0])
    u, w = st[1:4], st[8:11]
    re, rg = rot_rows(u), rot_rows(w)
    gap = [st[11 + i] - st[4 + i] for i in range(3)]
    d1 = mom[0:3]
    tx = [mom[3 + 3 * j : 6 + 3 * j] for j in range(3)]
    s0 = mom[16]
    s1 = mom[17:20]
    s2, dd = {}, {}
    for n, (i, j) in enumerate(SYM):
        s2[i, j] = s2[j, i] = mom[20 + n]
        dd[i, j] = dd[j, i] = mom[32 + n]
    sre = [[factor * re[i][j] for j in range(3)] for i in range(3)]

    def dot(left, right):
        return left[0] * right[0] + left[1] * right[1] + left[2] * right[2]

    shift = [2.0 * (dot(rg[i], d1) + gap[i] * s0 - dot(sre[i], s1)) for i in range(3)]
    mx = [
        [
            2.0
            * (
                dot(rg[i], [tx[j][k] for j in range(3)])
                + gap[i] * s1[k]
                - dot(sre[i], [s2[j, k] for j in range(3)])
            )
            for k in range(3)
        ]
        for i in range(3)
    ]
    mc = [
        [
            2.0
            * (
                dot(rg[i], [dd[j, k] for j in range(3)])
                + gap[i] * d1[k]
                - dot(sre[i], tx[k])
            )
            for k in range(3)
        ]
        for i in range(3)
    ]
    d_scale = -sum(mx[i][k] * sre[i][k] for i in range(3) for k in range(3))
    d_spin = rot_grad_rows(u, [[-factor * mx[i][k] for k in range(3)] for i in range(3)])
    d_turn = rot_grad_rows(w, mc)
    d_focal = -sum(rg[i][j] * mc[i][j] for i in range(3) for j in range(2))
    grads_p = jnp.concatenate([d_scale] + d_spin + [-x for x in shift] + [s0], 0)
    grads_i = jnp.concatenate([d_focal] + d_turn + shift + [s0], 0)
    grads_p = grads_p + swap(grads_p)
    grads_i = jnp.dot(
        grads_i,
        same,
        precision=lax.Precision.HIGHEST,
        preferred_element_type=jnp.float32,
    )
    rate_p = (0.05, 0.02, 0.02, 0.02, 0.3, 0.3, 0.3)
    rate_i = (0.1, 0.02, 0.02, 0.02, 0.3, 0.3, 0.3)
    down_p = 1.0 / (grads_p[7:8] + 1.0)
    down_i = 1.0 / (grads_i[7:8] + 1.0)
    new = [st[i] - rate_p[i] * grads_p[i : i + 1] * down_p for i in range(7)]
    new += [st[7 + i] - rate_i[i] * grads_i[i : i + 1] * down_i for i in range(7)]
    return new


def step_kernel(first, meta, rep, coef, own, far, z_ref, a_ref, b_ref, *rest):
    if first:
        z_out, mom_out, dc, total, weights = rest
    else:
        before, z_out, mom_out, dc, total, weights = rest
    images, rows, _ = z_ref.shape
    views = coef.shape[1]
    own_count, far_count = own.shape[0], meta.shape[1] - own.shape[0]
    lane = lax.broadcasted_iota(jnp.int32, (1, views), 1)
    whole = rows // CHUNK * CHUNK
    left = rows - whole
    cuts = [pl.ds(c * CHUNK, CHUNK) for c in range(rows // CHUNK)]
    if left:
        cuts.append(pl.ds(whole, left))

    mom_out[...] = jnp.zeros_like(mom_out)
    if not first:
        mom_out[16:32, :] = before[16:32, :]

    def half(x):
        if x.shape[0] == 16:
            return x[0:8] + x[8:16]
        if x.shape[0] > 8:
            more = jnp.zeros((16 - x.shape[0], LANES), jnp.float32)
            return x[0:8] + jnp.concatenate([x[8:], more], 0)
        if x.shape[0] == 8:
            return x
        return jnp.concatenate([x, jnp.zeros((8 - x.shape[0], LANES), jnp.float32)], 0)

    def fields(data, slot, cut):
        if cut.size == CHUNK:
            return [
                data[slot, pl.ds(k * whole + cut.start, CHUNK), :].astype(jnp.float32)
                for k in range(4)
            ]
        tail = data[slot, 4 * whole :, :].astype(jnp.float32)
        return [tail[k * left : (k + 1) * left] for k in range(4)]

    def put(row, sums, column):
        lines = [jnp.sum(x, 0, keepdims=True) for x in sums]
        count = -(-len(lines) // 8) * 8
        lines += [jnp.zeros_like(lines[0])] * (count - len(lines))
        value = jnp.sum(jnp.concatenate(lines, 0), 1, keepdims=True)
        mom_out[row : row + count, :] += jnp.where(lane == column, value, 0.0)

    def prepare(g, _):
        inv = coef[12, rep[g]]
        for cut in cuts:
            d = jnp.exp(z_ref[g, cut, :])
            near = d * inv
            dc[g, 0, cut, :] = near * a_ref[cut, :]
            dc[g, 1, cut, :] = near * b_ref[cut, :]
            dc[g, 2, cut, :] = d
            total[g, cut, :] = jnp.zeros((cut.size, LANES), jnp.float32)
            weights[g, cut, :] = jnp.zeros((cut.size, LANES), jnp.float32)
        return 0

    lax.fori_loop(0, images, prepare, 0)

    def view(data, slot, g, column):
        q = [[coef[3 * j + k, column] for k in range(3)] for j in range(3)]
        p = [coef[9 + j, column] for j in range(3)]
        sums = None
        consts = None
        for cut in cuts:
            *x, w = fields(data, slot, cut)
            y = [dc[g, j, cut, :] * w for j in range(3)]
            t = [[y[j] * x[k] for k in range(3)] for j in range(3)]
            pull = p[0] * y[0] + p[1] * y[1] + p[2] * y[2]
            for j in range(3):
                for k in range(3):
                    pull = pull + q[j][k] * t[j][k]
            total[g, cut, :] += pull
            weights[g, cut, :] += w
            new = [half(v) for v in y] + [half(t[j][k]) for j in range(3) for k in range(3)]
            sums = new if sums is None else [s + v for s, v in zip(sums, new)]
            if first:
                wx = [w * x[k] for k in range(3)]
                new = [half(w)] + [half(v) for v in wx]
                new += [half(wx[i] * x[j]) for i, j in SYM]
                consts = new if consts is None else [s + v for s, v in zip(consts, new)]
        put(0, sums, column)
        if first:
            put(16, consts, column)

    def own_view(i, _):
        view(own, meta[1, i], meta[2, i], meta[3, i])
        return 0

    lax.fori_loop(0, own_count, own_view, 0)

    def far_view(i, _):
        at = own_count + i

        @pl.when(meta[0, at] > 0)
        def _():
            view(far, meta[1, at], meta[2, at], meta[3, at])

        return 0

    lax.fori_loop(0, far_count, far_view, 0)

    def finish(g, _):
        sums = None
        for cut in cuts:
            c = [dc[g, j, cut, :] for j in range(3)]
            w = weights[g, cut, :]
            wc = [w * c[j] for j in range(3)]
            twice = 2.0 * (wc[0] * c[0] + wc[1] * c[1] + wc[2] * c[2])
            z_out[g, cut, :] = z_ref[g, cut, :] - (twice - 2.0 * total[g, cut, :]) / (twice + 1.0)
            new = [half(wc[i] * c[j]) for i, j in SYM]
            sums = new if sums is None else [s + v for s, v in zip(sums, new)]
        put(32, sums, rep[g])
        return 0

    lax.fori_loop(0, images, finish, 0)


def pack_kernel(place, maps, conf, own, send, wide):
    pairs, parts, rows, _, _ = maps.shape
    whole = rows // CHUNK * CHUNK
    left = rows - whole

    def pair(i, _):
        tails = [[], []]
        for k in range(parts + 1):
            both = maps[i, k] if k < parts else conf[i]
            wide[k, 0 : 2 * rows, :] = both.astype(jnp.float32).reshape(2 * rows, LANES)
            for v in range(2):
                body = wide[k, pl.ds(v, whole, stride=2), :].astype(jnp.bfloat16)
                if v == 0:
                    own[i, k * whole : (k + 1) * whole, :] = body
                else:
                    send[place[i], k * whole : (k + 1) * whole, :] = body
                if left:
                    tails[v].append(wide[k, pl.ds(2 * whole + v, left, stride=2), :])
        if left:
            start = (parts + 1) * whole
            spare = tail_rows(rows) - (parts + 1) * left
            for v in range(2):
                lines = tails[v]
                if spare:
                    lines = lines + [jnp.zeros((spare, LANES), jnp.float32)]
                tail = jnp.concatenate(lines, 0).astype(jnp.bfloat16)
                if v == 0:
                    own[i, start:, :] = tail
                else:
                    send[place[i], start:, :] = tail
        return 0

    lax.fori_loop(0, pairs, pair, 0)


def tail_rows(rows):
    return -(-4 * (rows % CHUNK) // CHUNK) * CHUNK


def run_pack(place, slots, maps, conf):
    pairs, parts, rows, _, _ = maps.shape
    high = (parts + 1) * (rows // CHUNK * CHUNK) + tail_rows(rows)
    smem = pl.BlockSpec(memory_space=pltpu.SMEM)
    vmem = pl.BlockSpec(memory_space=pltpu.VMEM)
    return pl.pallas_call(
        pack_kernel,
        out_shape=(
            jax.ShapeDtypeStruct((pairs, high, LANES), jnp.bfloat16),
            jax.ShapeDtypeStruct((slots, high, LANES), jnp.bfloat16),
        ),
        in_specs=[smem, vmem, vmem],
        out_specs=(vmem, vmem),
        scratch_shapes=[pltpu.VMEM((parts + 1, 2 * rows + 4, LANES), jnp.float32)],
        compiler_params=pltpu.CompilerParams(vmem_limit_bytes=48 * 1024 * 1024),
    )(place, maps, conf)


def run_step(first, meta, rep, coef, own, far, z, a, b, before):
    images, rows, _ = z.shape
    views = coef.shape[1]
    smem = pl.BlockSpec(memory_space=pltpu.SMEM)
    vmem = pl.BlockSpec(memory_space=pltpu.VMEM)
    args = [meta, rep, coef, own, far, z, a, b] + ([] if first else [before])
    return pl.pallas_call(
        functools.partial(step_kernel, first),
        out_shape=(
            jax.ShapeDtypeStruct(z.shape, jnp.float32),
            jax.ShapeDtypeStruct((ROWS, views), jnp.float32),
        ),
        in_specs=[smem] * 3 + [vmem] * (len(args) - 3),
        out_specs=(vmem, vmem),
        scratch_shapes=[
            pltpu.VMEM((images, 3, rows, LANES), jnp.float32),
            pltpu.VMEM((images, rows, LANES), jnp.float32),
            pltpu.VMEM((images, rows, LANES), jnp.float32),
        ],
        compiler_params=pltpu.CompilerParams(vmem_limit_bytes=32 * 1024 * 1024),
    )(*args)


def share_kernel(
    n_pair, n_img, mom, state, same, state_out, coef_out, buf1, buf2, s1, r1, s2, r2
):
    views = mom.shape[1]
    stages = (("pair", n_pair, buf1, s1, r1), ("img", n_img, buf2, s2, r2))
    barrier = pltpu.get_barrier_semaphore()
    for axis, size, _, _, _ in stages:
        me = lax.axis_index(axis)
        for k in range(1, size):
            peer = lax.rem(me + k, size)
            pl.semaphore_signal(barrier, inc=1, device_id={axis: peer}, device_id_type=MESH)
    pl.semaphore_wait(barrier, n_pair + n_img - 2)

    value = mom[...]
    for axis, size, buf, send, recv in stages:
        me = lax.axis_index(axis)
        buf[me] = value
        copies = []
        for k in range(1, size):
            peer = lax.rem(me + k, size)
            copy = pltpu.make_async_remote_copy(
                src_ref=buf.at[me],
                dst_ref=buf.at[me],
                send_sem=send.at[k],
                recv_sem=recv.at[me],
                device_id={axis: peer},
                device_id_type=MESH,
            )
            copy.start()
            copies.append(copy)
        for k in range(1, size):
            peer = lax.rem(me + k, size)
            pltpu.make_async_remote_copy(
                src_ref=buf.at[peer],
                dst_ref=buf.at[peer],
                send_sem=send.at[k],
                recv_sem=recv.at[peer],
                device_id={axis: peer},
                device_id_type=MESH,
            ).wait_recv()
        value = buf[0]
        for k in range(1, size):
            value = value + buf[k]
        for copy in copies:
            copy.wait_send()

    moments = [value[i : i + 1] for i in range(ROWS)]
    st = [state[i : i + 1, :] for i in range(14)]
    new = update_rows(st, moments, same[...], lambda x: pltpu.roll(x, views // 2, axis=1))
    zero = jnp.zeros_like(new[0])
    state_out[...] = jnp.concatenate(new + [zero] * 2, 0)
    coef_out[...] = jnp.concatenate(coef_rows(new), 0)


def run_share(n_pair, n_img, mom, state, same):
    views = mom.shape[1]
    vmem = pl.BlockSpec(memory_space=pltpu.VMEM)
    return pl.pallas_call(
        functools.partial(share_kernel, n_pair, n_img),
        out_shape=(
            jax.ShapeDtypeStruct((16, views), jnp.float32),
            jax.ShapeDtypeStruct((16, views), jnp.float32),
        ),
        in_specs=[vmem] * 3,
        out_specs=(vmem, vmem),
        scratch_shapes=[
            pltpu.VMEM((n_pair, ROWS, views), jnp.float32),
            pltpu.VMEM((n_img, ROWS, views), jnp.float32),
            pltpu.SemaphoreType.DMA((n_pair,)),
            pltpu.SemaphoreType.DMA((n_pair,)),
            pltpu.SemaphoreType.DMA((n_img,)),
            pltpu.SemaphoreType.DMA((n_img,)),
        ],
        compiler_params=pltpu.CompilerParams(collective_id=0, has_side_effects=True),
    )(mom, state, same)


def per_device(pair_images, pointmaps, confidence, log_depth, image_params, pair_params):
    pair_dev = pair_images.shape[0]
    img_dev, pix_dev = log_depth.shape
    blocks = lax.axis_size("img")
    n_pair = lax.axis_size("pair")
    slots = max(2, 2 * pair_dev // blocks)
    here = lax.axis_index("img")
    rows = pix_dev // LANES

    pixel = lax.axis_index("pair") * pix_dev + jnp.arange(rows * LANES)
    coord_a = ((pixel % SIDE).astype(jnp.float32) - (SIDE - 1) / 2.0) / SIDE
    coord_b = ((pixel // SIDE).astype(jnp.float32) - (SIDE - 1) / 2.0) / SIDE
    coord_a = coord_a.reshape(rows, LANES)
    coord_b = coord_b.reshape(rows, LANES)

    target = pair_images[:, 1] // img_dev
    hits = (target[:, None] == jnp.arange(blocks)[None, :]).astype(jnp.int32)
    rank = jnp.sum(jnp.cumsum(hits, 0) * hits, 1) - 1
    place = target * slots + rank
    maps = pointmaps.reshape(pair_dev, 2, 3, rows, LANES).transpose(0, 2, 3, 1, 4)
    conf = confidence.reshape(pair_dev, 2, rows, LANES).transpose(0, 2, 1, 3)
    own, send = run_pack(place.astype(jnp.int32), blocks * slots, maps, conf)
    high = own.shape[1]
    send = send.reshape(blocks, slots, high, LANES)
    far = lax.all_to_all(send, "img", split_axis=0, concat_axis=0, tiled=True)
    far = far.reshape(blocks * slots, high, LANES)

    small = jnp.concatenate(
        [
            pair_images.astype(jnp.float32).reshape(-1),
            pair_params.reshape(-1),
            image_params.reshape(-1),
        ]
    )
    small = lax.all_gather(small, "img")
    cut1, cut2 = 2 * pair_dev, 9 * pair_dev
    all_ids = small[:, :cut1].astype(jnp.int32).reshape(blocks * pair_dev, 2)
    all_pairs = small[:, cut1:cut2].reshape(blocks * pair_dev, 7)
    all_images = small[:, cut2:].reshape(blocks * img_dev, 7)
    image_of = all_ids.T.reshape(-1)
    views = image_of.shape[0]
    pairs = views // 2
    same = (image_of[:, None] == image_of[None, :]).astype(jnp.float32)
    hot = (image_of[None, :] == jnp.arange(blocks * img_dev)[:, None]).astype(jnp.float32)
    by_view = jnp.dot(
        all_images.T, hot, precision=lax.Precision.HIGHEST, preferred_element_type=jnp.float32
    )
    state = jnp.concatenate(
        [jnp.tile(all_pairs.T, (1, 2)), by_view, jnp.zeros((2, views), jnp.float32)], 0
    )
    coef = jnp.concatenate(coef_rows([state[i : i + 1] for i in range(14)]), 0)

    far_ids = all_ids[:, 1].reshape(blocks, pair_dev)
    mine = (far_ids // img_dev == here).astype(jnp.int32)
    far_slot = jnp.arange(blocks)[:, None] * slots + jnp.cumsum(mine, 1) - 1
    mine = mine.reshape(-1)
    meta = jnp.stack(
        [
            jnp.concatenate([jnp.ones((pair_dev,), jnp.int32), mine]),
            jnp.concatenate([jnp.arange(pair_dev), jnp.maximum(far_slot.reshape(-1), 0)]),
            jnp.concatenate([pair_images[:, 0] - here * img_dev, far_ids.reshape(-1) % img_dev]),
            jnp.concatenate([here * pair_dev + jnp.arange(pair_dev), pairs + jnp.arange(pairs)]),
        ]
    ).astype(jnp.int32)
    local = image_of[None, :] == here * img_dev + jnp.arange(img_dev)[:, None]
    rep = jnp.max(jnp.where(local, jnp.arange(views)[None, :], -1), 1)
    seen = rep >= 0
    rep = jnp.maximum(rep, 0).astype(jnp.int32)

    z = log_depth.reshape(img_dev, rows, LANES)
    before = None
    for step in range(STEPS):
        z, mom = run_step(step == 0, meta, rep, coef, own, far, z, coord_a, coord_b, before)
        before = mom
        state, coef = run_share(n_pair, blocks, mom, state, same)

    new_depth = z.reshape(img_dev, pix_dev)
    new_pairs = lax.dynamic_slice(state, (0, here * pair_dev), (7, pair_dev)).T
    new_images = jnp.where(seen[:, None], state[7:14][:, rep].T, image_params)
    return (new_depth, new_images, new_pairs)


def solution(mesh):
    in_specs = (
        P(("groups", "img"), None),
        P(("groups", "img"), None, None, "pair"),
        P(("groups", "img"), None, "pair"),
        P(("groups", "img"), "pair"),
        P(("groups", "img"), None),
        P(("groups", "img"), None),
    )
    out_specs = (
        P(("groups", "img"), "pair"),
        P(("groups", "img"), None),
        P(("groups", "img"), None),
    )
    return jax.shard_map(
        per_device, mesh=mesh, in_specs=in_specs, out_specs=out_specs, check_vma=False
    )
```

```python
import functools

import jax
import jax.numpy as jnp
from jax import lax
from jax.experimental import pallas as pl
from jax.experimental.pallas import tpu as pltpu
from jax.sharding import PartitionSpec as P

SIDE = 224
STEPS = 3
LANES = 128
CHUNK = 16
MESH = pl.DeviceIdType.MESH
ROWS = 40
SYM = ((0, 0), (0, 1), (0, 2), (1, 1), (1, 2), (2, 2))


def rot_rows(w):
    norm = w[0] * w[0] + w[1] * w[1] + w[2] * w[2]
    k = 2.0 / (1.0 + norm)
    cross = [[None, -w[2], w[1]], [w[2], None, -w[0]], [-w[1], w[0], None]]
    out = []
    for i in range(3):
        line = []
        for j in range(3):
            if i == j:
                line.append(1.0 + k * (w[i] * w[i] - norm))
            else:
                line.append(k * (cross[i][j] + w[i] * w[j]))
        out.append(line)
    return out


def rot_grad_rows(w, g):
    norm = w[0] * w[0] + w[1] * w[1] + w[2] * w[2]
    k = 2.0 / (1.0 + norm)
    trace = g[0][0] + g[1][1] + g[2][2]
    skew = [g[2][1] - g[1][2], g[0][2] - g[2][0], g[1][0] - g[0][1]]
    lin = [sum(g[i][j] * w[j] for j in range(3)) for i in range(3)]
    both = [lin[i] + sum(g[j][i] * w[j] for j in range(3)) for i in range(3)]
    value = sum(w[i] * (skew[i] + lin[i]) for i in range(3)) - norm * trace
    return [
        k * (skew[i] + both[i] - 2.0 * w[i] * trace) - k * k * w[i] * value for i in range(3)
    ]


def coef_rows(st):
    factor = jnp.exp(st[0])
    re = rot_rows(st[1:4])
    rg = rot_rows(st[8:11])
    gap = [st[4 + i] - st[11 + i] for i in range(3)]
    rows = []
    for j in range(3):
        for k in range(3):
            rows.append(factor * sum(rg[i][j] * re[i][k] for i in range(3)))
    for j in range(3):
        rows.append(sum(rg[i][j] * gap[i] for i in range(3)))
    rows.append(jnp.exp(-st[7]))
    zero = jnp.zeros_like(rows[0])
    return rows + [zero] * 3


def update_rows(st, mom, same, swap):
    factor = jnp.exp(st[0])
    u, w = st[1:4], st[8:11]
    re, rg = rot_rows(u), rot_rows(w)
    gap = [st[11 + i] - st[4 + i] for i in range(3)]
    d1 = mom[0:3]
    tx = [mom[3 + 3 * j : 6 + 3 * j] for j in range(3)]
    s0 = mom[16]
    s1 = mom[17:20]
    s2, dd = {}, {}
    for n, (i, j) in enumerate(SYM):
        s2[i, j] = s2[j, i] = mom[20 + n]
        dd[i, j] = dd[j, i] = mom[32 + n]
    sre = [[factor * re[i][j] for j in range(3)] for i in range(3)]

    def dot(left, right):
        return left[0] * right[0] + left[1] * right[1] + left[2] * right[2]

    shift = [2.0 * (dot(rg[i], d1) + gap[i] * s0 - dot(sre[i], s1)) for i in range(3)]
    mx = [
        [
            2.0
            * (
                dot(rg[i], [tx[j][k] for j in range(3)])
                + gap[i] * s1[k]
                - dot(sre[i], [s2[j, k] for j in range(3)])
            )
            for k in range(3)
        ]
        for i in range(3)
    ]
    mc = [
        [
            2.0
            * (
                dot(rg[i], [dd[j, k] for j in range(3)])
                + gap[i] * d1[k]
                - dot(sre[i], tx[k])
            )
            for k in range(3)
        ]
        for i in range(3)
    ]
    d_scale = -sum(mx[i][k] * sre[i][k] for i in range(3) for k in range(3))
    d_spin = rot_grad_rows(u, [[-factor * mx[i][k] for k in range(3)] for i in range(3)])
    d_turn = rot_grad_rows(w, mc)
    d_focal = -sum(rg[i][j] * mc[i][j] for i in range(3) for j in range(2))
    grads_p = jnp.concatenate([d_scale] + d_spin + [-x for x in shift] + [s0], 0)
    grads_i = jnp.concatenate([d_focal] + d_turn + shift + [s0], 0)
    grads_p = grads_p + swap(grads_p)
    grads_i = jnp.dot(
        grads_i,
        same,
        precision=lax.Precision.HIGHEST,
        preferred_element_type=jnp.float32,
    )
    rate_p = (0.05, 0.02, 0.02, 0.02, 0.3, 0.3, 0.3)
    rate_i = (0.1, 0.02, 0.02, 0.02, 0.3, 0.3, 0.3)
    down_p = 1.0 / (grads_p[7:8] + 1.0)
    down_i = 1.0 / (grads_i[7:8] + 1.0)
    new = [st[i] - rate_p[i] * grads_p[i : i + 1] * down_p for i in range(7)]
    new += [st[7 + i] - rate_i[i] * grads_i[i : i + 1] * down_i for i in range(7)]
    return new


def step_kernel(mode, own_count, meta, rep, coef, z_ref, a_ref, b_ref, *rest):
    first = mode != "all"
    if mode == "own":
        own, total, weights, mom_out, dc = rest
    elif mode == "far":
        far, total_in, weights_in, before, z_out, weights, mom_out, dc, total = rest
    else:
        own, far, weights, before, z_out, mom_out, dc, total = rest
    images, rows, _ = z_ref.shape
    views = coef.shape[1]
    far_count = meta.shape[1] - own_count
    lane = lax.broadcasted_iota(jnp.int32, (1, views), 1)
    whole = rows // CHUNK * CHUNK
    left = rows - whole
    cuts = [pl.ds(c * CHUNK, CHUNK) for c in range(rows // CHUNK)]
    if left:
        cuts.append(pl.ds(whole, left))

    if mode == "far":
        mom_out[...] = before[...]
        total[...] = total_in[...]
        weights[...] = weights_in[...]
    else:
        mom_out[...] = jnp.zeros_like(mom_out)
        total[...] = jnp.zeros_like(total)
        if mode == "own":
            weights[...] = jnp.zeros_like(weights)
        else:
            mom_out[16:32, :] = before[16:32, :]

    def half(x):
        if x.shape[0] == 16:
            return x[0:8] + x[8:16]
        if x.shape[0] > 8:
            more = jnp.zeros((16 - x.shape[0], LANES), jnp.float32)
            return x[0:8] + jnp.concatenate([x[8:], more], 0)
        if x.shape[0] == 8:
            return x
        return jnp.concatenate([x, jnp.zeros((8 - x.shape[0], LANES), jnp.float32)], 0)

    def fields(data, slot, cut):
        if cut.size == CHUNK:
            return [
                data[slot, pl.ds(k * whole + cut.start, CHUNK), :].astype(jnp.float32)
                for k in range(4)
            ]
        tail = data[slot, 4 * whole :, :].astype(jnp.float32)
        return [tail[k * left : (k + 1) * left] for k in range(4)]

    def put(row, sums, column):
        lines = [jnp.sum(x, 0, keepdims=True) for x in sums]
        count = -(-len(lines) // 8) * 8
        lines += [jnp.zeros_like(lines[0])] * (count - len(lines))
        value = jnp.sum(jnp.concatenate(lines, 0), 1, keepdims=True)
        mom_out[row : row + count, :] += jnp.where(lane == column, value, 0.0)

    def prepare(g, _):
        inv = coef[12, rep[g]]
        for cut in cuts:
            d = jnp.exp(z_ref[g, cut, :])
            near = d * inv
            dc[g, 0, cut, :] = near * a_ref[cut, :]
            dc[g, 1, cut, :] = near * b_ref[cut, :]
            dc[g, 2, cut, :] = d
        return 0

    lax.fori_loop(0, images, prepare, 0)

    def view(data, slot, g, column):
        q = [[coef[3 * j + k, column] for k in range(3)] for j in range(3)]
        p = [coef[9 + j, column] for j in range(3)]
        sums = None
        consts = None
        for cut in cuts:
            *x, w = fields(data, slot, cut)
            y = [dc[g, j, cut, :] * w for j in range(3)]
            t = [[y[j] * x[k] for k in range(3)] for j in range(3)]
            pull = p[0] * y[0] + p[1] * y[1] + p[2] * y[2]
            for j in range(3):
                for k in range(3):
                    pull = pull + q[j][k] * t[j][k]
            total[g, cut, :] += pull
            if first:
                weights[g, cut, :] += w
            new = [half(v) for v in y] + [half(t[j][k]) for j in range(3) for k in range(3)]
            sums = new if sums is None else [s + v for s, v in zip(sums, new)]
            if first:
                wx = [w * x[k] for k in range(3)]
                new = [half(w)] + [half(v) for v in wx]
                new += [half(wx[i] * x[j]) for i, j in SYM]
                consts = new if consts is None else [s + v for s, v in zip(consts, new)]
        put(0, sums, column)
        if first:
            put(16, consts, column)

    def own_view(i, _):
        view(own, meta[1, i], meta[2, i], meta[3, i])
        return 0

    if mode != "far":
        lax.fori_loop(0, own_count, own_view, 0)
    if mode == "own":
        return

    def far_view(i, _):
        at = own_count + i

        @pl.when(meta[0, at] > 0)
        def _():
            view(far, meta[1, at], meta[2, at], meta[3, at])

        return 0

    lax.fori_loop(0, far_count, far_view, 0)

    def finish(g, _):
        sums = None
        for cut in cuts:
            c = [dc[g, j, cut, :] for j in range(3)]
            w = weights[g, cut, :]
            wc = [w * c[j] for j in range(3)]
            twice = 2.0 * (wc[0] * c[0] + wc[1] * c[1] + wc[2] * c[2])
            z_out[g, cut, :] = z_ref[g, cut, :] - (twice - 2.0 * total[g, cut, :]) / (twice + 1.0)
            new = [half(wc[i] * c[j]) for i, j in SYM]
            sums = new if sums is None else [s + v for s, v in zip(sums, new)]
        put(32, sums, rep[g])
        return 0

    lax.fori_loop(0, images, finish, 0)


def pack_kernel(place, maps, conf, own, send, wide):
    pairs, parts, rows, _, _ = maps.shape
    whole = rows // CHUNK * CHUNK
    left = rows - whole

    def pair(i, _):
        tails = [[], []]
        for k in range(parts + 1):
            both = maps[i, k] if k < parts else conf[i]
            wide[k, 0 : 2 * rows, :] = both.astype(jnp.float32).reshape(2 * rows, LANES)
            for v in range(2):
                body = wide[k, pl.ds(v, whole, stride=2), :].astype(jnp.bfloat16)
                if v == 0:
                    own[i, k * whole : (k + 1) * whole, :] = body
                else:
                    send[place[i], k * whole : (k + 1) * whole, :] = body
                if left:
                    tails[v].append(wide[k, pl.ds(2 * whole + v, left, stride=2), :])
        if left:
            start = (parts + 1) * whole
            spare = tail_rows(rows) - (parts + 1) * left
            for v in range(2):
                lines = tails[v]
                if spare:
                    lines = lines + [jnp.zeros((spare, LANES), jnp.float32)]
                tail = jnp.concatenate(lines, 0).astype(jnp.bfloat16)
                if v == 0:
                    own[i, start:, :] = tail
                else:
                    send[place[i], start:, :] = tail
        return 0

    lax.fori_loop(0, pairs, pair, 0)


def tail_rows(rows):
    return -(-4 * (rows % CHUNK) // CHUNK) * CHUNK


def run_pack(place, slots, maps, conf):
    pairs, parts, rows, _, _ = maps.shape
    high = (parts + 1) * (rows // CHUNK * CHUNK) + tail_rows(rows)
    smem = pl.BlockSpec(memory_space=pltpu.SMEM)
    vmem = pl.BlockSpec(memory_space=pltpu.VMEM)
    return pl.pallas_call(
        pack_kernel,
        out_shape=(
            jax.ShapeDtypeStruct((pairs, high, LANES), jnp.bfloat16),
            jax.ShapeDtypeStruct((slots, high, LANES), jnp.bfloat16),
        ),
        in_specs=[smem, vmem, vmem],
        out_specs=(vmem, vmem),
        scratch_shapes=[pltpu.VMEM((parts + 1, 2 * rows + 4, LANES), jnp.float32)],
        compiler_params=pltpu.CompilerParams(vmem_limit_bytes=20 * 1024 * 1024),
    )(place, maps, conf)


def run_step(mode, own_count, meta, rep, coef, z, a, b, *rest):
    images, rows, _ = z.shape
    views = coef.shape[1]
    smem = pl.BlockSpec(memory_space=pltpu.SMEM)
    vmem = pl.BlockSpec(memory_space=pltpu.VMEM)
    field = jax.ShapeDtypeStruct(z.shape, jnp.float32)
    moments = jax.ShapeDtypeStruct((ROWS, views), jnp.float32)
    outs = {"own": (field, field, moments), "far": (field, field, moments), "all": (field, moments)}
    scratch = [pltpu.VMEM((images, 3, rows, LANES), jnp.float32)]
    if mode != "own":
        scratch.append(pltpu.VMEM((images, rows, LANES), jnp.float32))
    return pl.pallas_call(
        functools.partial(step_kernel, mode, own_count),
        out_shape=outs[mode],
        in_specs=[smem] * 3 + [vmem] * (3 + len(rest)),
        out_specs=tuple(vmem for _ in outs[mode]),
        scratch_shapes=scratch,
        compiler_params=pltpu.CompilerParams(vmem_limit_bytes=20 * 1024 * 1024),
        cost_estimate=pl.CostEstimate(
            flops=16 * 1024 * 1024 * 8, bytes_accessed=8 * 1024 * 1024, transcendentals=0
        ),
    )(meta, rep, coef, z, a, b, *rest)


def spread_kernel(size, small, out, send, recv):
    me = lax.axis_index("img")
    barrier = pltpu.get_barrier_semaphore()
    for k in range(1, size):
        peer = lax.rem(me + k, size)
        pl.semaphore_signal(barrier, inc=1, device_id={"img": peer}, device_id_type=MESH)
    pl.semaphore_wait(barrier, size - 1)
    copies = []
    for k in range(1, size):
        peer = lax.rem(me + k, size)
        copy = pltpu.make_async_remote_copy(
            src_ref=small,
            dst_ref=out.at[me],
            send_sem=send.at[k],
            recv_sem=recv.at[me],
            device_id={"img": peer},
            device_id_type=MESH,
        )
        copy.start()
        copies.append(copy)
    out[me] = small[...]
    for k in range(1, size):
        peer = lax.rem(me + k, size)
        pltpu.make_async_remote_copy(
            src_ref=small,
            dst_ref=out.at[peer],
            send_sem=send.at[k],
            recv_sem=recv.at[peer],
            device_id={"img": peer},
            device_id_type=MESH,
        ).wait_recv()
    for copy in copies:
        copy.wait_send()


def run_spread(size, small):
    vmem = pl.BlockSpec(memory_space=pltpu.VMEM)
    return pl.pallas_call(
        functools.partial(spread_kernel, size),
        out_shape=jax.ShapeDtypeStruct((size,) + small.shape, jnp.float32),
        in_specs=[vmem],
        out_specs=vmem,
        scratch_shapes=[pltpu.SemaphoreType.DMA((size,)), pltpu.SemaphoreType.DMA((size,))],
        compiler_params=pltpu.CompilerParams(
            collective_id=1, has_side_effects=True, vmem_limit_bytes=2 * 1024 * 1024
        ),
    )(small)


def share_kernel(
    n_pair, n_img, mom, state, same, state_out, coef_out, buf1, buf2, s1, r1, s2, r2
):
    views = mom.shape[1]
    stages = (("pair", n_pair, buf1, s1, r1), ("img", n_img, buf2, s2, r2))
    barrier = pltpu.get_barrier_semaphore()
    for axis, size, _, _, _ in stages:
        me = lax.axis_index(axis)
        for k in range(1, size):
            peer = lax.rem(me + k, size)
            pl.semaphore_signal(barrier, inc=1, device_id={axis: peer}, device_id_type=MESH)
    pl.semaphore_wait(barrier, n_pair + n_img - 2)

    value = mom[...]
    for axis, size, buf, send, recv in stages:
        me = lax.axis_index(axis)
        buf[me] = value
        copies = []
        for k in range(1, size):
            peer = lax.rem(me + k, size)
            copy = pltpu.make_async_remote_copy(
                src_ref=buf.at[me],
                dst_ref=buf.at[me],
                send_sem=send.at[k],
                recv_sem=recv.at[me],
                device_id={axis: peer},
                device_id_type=MESH,
            )
            copy.start()
            copies.append(copy)
        for k in range(1, size):
            peer = lax.rem(me + k, size)
            pltpu.make_async_remote_copy(
                src_ref=buf.at[peer],
                dst_ref=buf.at[peer],
                send_sem=send.at[k],
                recv_sem=recv.at[peer],
                device_id={axis: peer},
                device_id_type=MESH,
            ).wait_recv()
        value = buf[0]
        for k in range(1, size):
            value = value + buf[k]
        for copy in copies:
            copy.wait_send()

    moments = [value[i : i + 1] for i in range(ROWS)]
    st = [state[i : i + 1, :] for i in range(14)]
    new = update_rows(st, moments, same[...], lambda x: pltpu.roll(x, views // 2, axis=1))
    zero = jnp.zeros_like(new[0])
    state_out[...] = jnp.concatenate(new + [zero] * 2, 0)
    coef_out[...] = jnp.concatenate(coef_rows(new), 0)


def run_share(n_pair, n_img, mom, state, same):
    views = mom.shape[1]
    vmem = pl.BlockSpec(memory_space=pltpu.VMEM)
    return pl.pallas_call(
        functools.partial(share_kernel, n_pair, n_img),
        out_shape=(
            jax.ShapeDtypeStruct((16, views), jnp.float32),
            jax.ShapeDtypeStruct((16, views), jnp.float32),
        ),
        in_specs=[vmem] * 3,
        out_specs=(vmem, vmem),
        scratch_shapes=[
            pltpu.VMEM((n_pair, ROWS, views), jnp.float32),
            pltpu.VMEM((n_img, ROWS, views), jnp.float32),
            pltpu.SemaphoreType.DMA((n_pair,)),
            pltpu.SemaphoreType.DMA((n_pair,)),
            pltpu.SemaphoreType.DMA((n_img,)),
            pltpu.SemaphoreType.DMA((n_img,)),
        ],
        compiler_params=pltpu.CompilerParams(
            collective_id=0, has_side_effects=True, vmem_limit_bytes=8 * 1024 * 1024
        ),
    )(mom, state, same)


def per_device(pair_images, pointmaps, confidence, log_depth, image_params, pair_params):
    pair_dev = pair_images.shape[0]
    img_dev, pix_dev = log_depth.shape
    blocks = lax.axis_size("img")
    n_pair = lax.axis_size("pair")
    slots = max(2, 2 * pair_dev // blocks)
    here = lax.axis_index("img")
    rows = pix_dev // LANES

    pixel = lax.axis_index("pair") * pix_dev + jnp.arange(rows * LANES)
    coord_a = ((pixel % SIDE).astype(jnp.float32) - (SIDE - 1) / 2.0) / SIDE
    coord_b = ((pixel // SIDE).astype(jnp.float32) - (SIDE - 1) / 2.0) / SIDE
    coord_a = coord_a.reshape(rows, LANES)
    coord_b = coord_b.reshape(rows, LANES)

    target = pair_images[:, 1] // img_dev
    hits = (target[:, None] == jnp.arange(blocks)[None, :]).astype(jnp.int32)
    rank = jnp.sum(jnp.cumsum(hits, 0) * hits, 1) - 1
    place = target * slots + rank
    small = jnp.concatenate(
        [
            pair_images.astype(jnp.float32).reshape(-1),
            pair_params.reshape(-1),
            image_params.reshape(-1),
        ]
    )
    count = small.shape[0]
    tiles = -(-count // (8 * LANES))
    small = jnp.pad(small, (0, tiles * 8 * LANES - count)).reshape(tiles * 8, LANES)
    small = run_spread(blocks, small)

    maps = pointmaps.reshape(pair_dev, 2, 3, rows, LANES).transpose(0, 2, 3, 1, 4)
    conf = confidence.reshape(pair_dev, 2, rows, LANES).transpose(0, 2, 1, 3)
    own, send = run_pack(place.astype(jnp.int32), blocks * slots, maps, conf)
    high = own.shape[1]
    small, send = lax.optimization_barrier((small, send))
    small = small.reshape(blocks, -1)[:, :count]
    send = send.reshape(blocks, slots, high, LANES)
    far = lax.all_to_all(send, "img", split_axis=0, concat_axis=0, tiled=True)
    far = far.reshape(blocks * slots, high, LANES)

    cut1, cut2 = 2 * pair_dev, 9 * pair_dev
    all_ids = small[:, :cut1].astype(jnp.int32).reshape(blocks * pair_dev, 2)
    all_pairs = small[:, cut1:cut2].reshape(blocks * pair_dev, 7)
    all_images = small[:, cut2:].reshape(blocks * img_dev, 7)
    image_of = all_ids.T.reshape(-1)
    views = image_of.shape[0]
    pairs = views // 2
    same = (image_of[:, None] == image_of[None, :]).astype(jnp.float32)
    hot = (image_of[None, :] == jnp.arange(blocks * img_dev)[:, None]).astype(jnp.float32)
    by_view = jnp.dot(
        all_images.T, hot, precision=lax.Precision.HIGHEST, preferred_element_type=jnp.float32
    )
    state = jnp.concatenate(
        [jnp.tile(all_pairs.T, (1, 2)), by_view, jnp.zeros((2, views), jnp.float32)], 0
    )
    coef = jnp.concatenate(coef_rows([state[i : i + 1] for i in range(14)]), 0)

    far_ids = all_ids[:, 1].reshape(blocks, pair_dev)
    mine = (far_ids // img_dev == here).astype(jnp.int32)
    far_slot = jnp.arange(blocks)[:, None] * slots + jnp.cumsum(mine, 1) - 1
    mine = mine.reshape(-1)
    meta = jnp.stack(
        [
            jnp.concatenate([jnp.ones((pair_dev,), jnp.int32), mine]),
            jnp.concatenate([jnp.arange(pair_dev), jnp.maximum(far_slot.reshape(-1), 0)]),
            jnp.concatenate([pair_images[:, 0] - here * img_dev, far_ids.reshape(-1) % img_dev]),
            jnp.concatenate([here * pair_dev + jnp.arange(pair_dev), pairs + jnp.arange(pairs)]),
        ]
    ).astype(jnp.int32)
    local = image_of[None, :] == here * img_dev + jnp.arange(img_dev)[:, None]
    rep = jnp.max(jnp.where(local, jnp.arange(views)[None, :], -1), 1)
    seen = rep >= 0
    rep = jnp.maximum(rep, 0).astype(jnp.int32)

    z = log_depth.reshape(img_dev, rows, LANES)
    head = (pair_dev, meta, rep)
    tail = (coord_a, coord_b)
    total, weights, mom = run_step("own", *head, coef, z, *tail, own)
    z, weights, mom = run_step("far", *head, coef, z, *tail, far, total, weights, mom)
    state, coef = run_share(n_pair, blocks, mom, state, same)
    for step in range(1, STEPS):
        z, mom = run_step("all", *head, coef, z, *tail, own, far, weights, mom)
        state, coef = run_share(n_pair, blocks, mom, state, same)

    new_depth = z.reshape(img_dev, pix_dev)
    new_pairs = lax.dynamic_slice(state, (0, here * pair_dev), (7, pair_dev)).T
    new_images = jnp.where(seen[:, None], state[7:14][:, rep].T, image_params)
    return (new_depth, new_images, new_pairs)


def solution(mesh):
    in_specs = (
        P(("groups", "img"), None),
        P(("groups", "img"), None, None, "pair"),
        P(("groups", "img"), None, "pair"),
        P(("groups", "img"), "pair"),
        P(("groups", "img"), None),
        P(("groups", "img"), None),
    )
    out_specs = (
        P(("groups", "img"), "pair"),
        P(("groups", "img"), None),
        P(("groups", "img"), None),
    )
    return jax.shard_map(
        per_device, mesh=mesh, in_specs=in_specs, out_specs=out_specs, check_vma=False
    )
```

```python
import functools

import jax
import jax.numpy as jnp
from jax import lax
from jax.experimental import pallas as pl
from jax.experimental.pallas import tpu as pltpu
from jax.sharding import PartitionSpec as P

SIDE = 224
STEPS = 3
LANES = 128
CHUNK = 16
MESH = pl.DeviceIdType.MESH
ROWS = 40
SYM = ((0, 0), (0, 1), (0, 2), (1, 1), (1, 2), (2, 2))


def rot_rows(w):
    norm = w[0] * w[0] + w[1] * w[1] + w[2] * w[2]
    k = 2.0 / (1.0 + norm)
    cross = [[None, -w[2], w[1]], [w[2], None, -w[0]], [-w[1], w[0], None]]
    out = []
    for i in range(3):
        line = []
        for j in range(3):
            if i == j:
                line.append(1.0 + k * (w[i] * w[i] - norm))
            else:
                line.append(k * (cross[i][j] + w[i] * w[j]))
        out.append(line)
    return out


def rot_grad_rows(w, g):
    norm = w[0] * w[0] + w[1] * w[1] + w[2] * w[2]
    k = 2.0 / (1.0 + norm)
    trace = g[0][0] + g[1][1] + g[2][2]
    skew = [g[2][1] - g[1][2], g[0][2] - g[2][0], g[1][0] - g[0][1]]
    lin = [sum(g[i][j] * w[j] for j in range(3)) for i in range(3)]
    both = [lin[i] + sum(g[j][i] * w[j] for j in range(3)) for i in range(3)]
    value = sum(w[i] * (skew[i] + lin[i]) for i in range(3)) - norm * trace
    return [
        k * (skew[i] + both[i] - 2.0 * w[i] * trace) - k * k * w[i] * value for i in range(3)
    ]


def coef_rows(st):
    factor = jnp.exp(st[0])
    re = rot_rows(st[1:4])
    rg = rot_rows(st[8:11])
    gap = [st[4 + i] - st[11 + i] for i in range(3)]
    rows = []
    for j in range(3):
        for k in range(3):
            rows.append(factor * sum(rg[i][j] * re[i][k] for i in range(3)))
    for j in range(3):
        rows.append(sum(rg[i][j] * gap[i] for i in range(3)))
    rows.append(jnp.exp(-st[7]))
    zero = jnp.zeros_like(rows[0])
    return rows + [zero] * 3


def update_rows(st, mom, same, swap):
    factor = jnp.exp(st[0])
    u, w = st[1:4], st[8:11]
    re, rg = rot_rows(u), rot_rows(w)
    gap = [st[11 + i] - st[4 + i] for i in range(3)]
    d1 = mom[0:3]
    tx = [mom[3 + 3 * j : 6 + 3 * j] for j in range(3)]
    s0 = mom[16]
    s1 = mom[17:20]
    s2, dd = {}, {}
    for n, (i, j) in enumerate(SYM):
        s2[i, j] = s2[j, i] = mom[20 + n]
        dd[i, j] = dd[j, i] = mom[32 + n]
    sre = [[factor * re[i][j] for j in range(3)] for i in range(3)]

    def dot(left, right):
        return left[0] * right[0] + left[1] * right[1] + left[2] * right[2]

    shift = [2.0 * (dot(rg[i], d1) + gap[i] * s0 - dot(sre[i], s1)) for i in range(3)]
    mx = [
        [
            2.0
            * (
                dot(rg[i], [tx[j][k] for j in range(3)])
                + gap[i] * s1[k]
                - dot(sre[i], [s2[j, k] for j in range(3)])
            )
            for k in range(3)
        ]
        for i in range(3)
    ]
    mc = [
        [
            2.0
            * (
                dot(rg[i], [dd[j, k] for j in range(3)])
                + gap[i] * d1[k]
                - dot(sre[i], tx[k])
            )
            for k in range(3)
        ]
        for i in range(3)
    ]
    d_scale = -sum(mx[i][k] * sre[i][k] for i in range(3) for k in range(3))
    d_spin = rot_grad_rows(u, [[-factor * mx[i][k] for k in range(3)] for i in range(3)])
    d_turn = rot_grad_rows(w, mc)
    d_focal = -sum(rg[i][j] * mc[i][j] for i in range(3) for j in range(2))
    grads_p = jnp.concatenate([d_scale] + d_spin + [-x for x in shift] + [s0], 0)
    grads_i = jnp.concatenate([d_focal] + d_turn + shift + [s0], 0)
    grads_p = grads_p + swap(grads_p)
    grads_i = jnp.dot(
        grads_i,
        same,
        precision=lax.Precision.HIGHEST,
        preferred_element_type=jnp.float32,
    )
    rate_p = (0.05, 0.02, 0.02, 0.02, 0.3, 0.3, 0.3)
    rate_i = (0.1, 0.02, 0.02, 0.02, 0.3, 0.3, 0.3)
    down_p = 1.0 / (grads_p[7:8] + 1.0)
    down_i = 1.0 / (grads_i[7:8] + 1.0)
    new = [st[i] - rate_p[i] * grads_p[i : i + 1] * down_p for i in range(7)]
    new += [st[7 + i] - rate_i[i] * grads_i[i : i + 1] * down_i for i in range(7)]
    return new


def step_kernel(mode, own_count, meta, rep, coef, z_ref, a_ref, b_ref, *rest):
    first = mode != "all"
    if mode == "own":
        own, total, weights, mom_out, dc = rest
    elif mode == "far":
        far, total_in, weights_in, before, z_out, weights, mom_out, dc, total = rest
    else:
        own, far, weights, before, z_out, mom_out, dc, total = rest
    images, rows, _ = z_ref.shape
    views = coef.shape[1]
    far_count = meta.shape[1] - own_count
    lane = lax.broadcasted_iota(jnp.int32, (1, views), 1)
    whole = rows // CHUNK * CHUNK
    left = rows - whole
    cuts = [pl.ds(c * CHUNK, CHUNK) for c in range(rows // CHUNK)]
    if left:
        cuts.append(pl.ds(whole, left))

    if mode == "far":
        mom_out[...] = before[...]
        total[...] = total_in[...]
        weights[...] = weights_in[...]
    else:
        mom_out[...] = jnp.zeros_like(mom_out)
        total[...] = jnp.zeros_like(total)
        if mode == "own":
            weights[...] = jnp.zeros_like(weights)
        else:
            mom_out[16:32, :] = before[16:32, :]

    def half(x):
        if x.shape[0] == 16:
            return x[0:8] + x[8:16]
        if x.shape[0] > 8:
            more = jnp.zeros((16 - x.shape[0], LANES), jnp.float32)
            return x[0:8] + jnp.concatenate([x[8:], more], 0)
        if x.shape[0] == 8:
            return x
        return jnp.concatenate([x, jnp.zeros((8 - x.shape[0], LANES), jnp.float32)], 0)

    def fields(data, slot, cut):
        if cut.size == CHUNK:
            return [
                data[slot, pl.ds(k * whole + cut.start, CHUNK), :].astype(jnp.float32)
                for k in range(4)
            ]
        tail = data[slot, 4 * whole :, :].astype(jnp.float32)
        return [tail[k * left : (k + 1) * left] for k in range(4)]

    def put(row, sums, column):
        lines = [jnp.sum(x, 0, keepdims=True) for x in sums]
        count = -(-len(lines) // 8) * 8
        lines += [jnp.zeros_like(lines[0])] * (count - len(lines))
        value = jnp.sum(jnp.concatenate(lines, 0), 1, keepdims=True)
        mom_out[row : row + count, :] += jnp.where(lane == column, value, 0.0)

    def prepare(g, _):
        inv = coef[12, rep[g]]
        for cut in cuts:
            d = jnp.exp(z_ref[g, cut, :])
            near = d * inv
            dc[g, 0, cut, :] = near * a_ref[cut, :]
            dc[g, 1, cut, :] = near * b_ref[cut, :]
            dc[g, 2, cut, :] = d
        return 0

    lax.fori_loop(0, images, prepare, 0)

    def view(data, slot, g, column):
        q = [[coef[3 * j + k, column] for k in range(3)] for j in range(3)]
        p = [coef[9 + j, column] for j in range(3)]
        sums = None
        consts = None
        for cut in cuts:
            *x, w = fields(data, slot, cut)
            y = [dc[g, j, cut, :] * w for j in range(3)]
            t = [[y[j] * x[k] for k in range(3)] for j in range(3)]
            pull = p[0] * y[0] + p[1] * y[1] + p[2] * y[2]
            for j in range(3):
                for k in range(3):
                    pull = pull + q[j][k] * t[j][k]
            total[g, cut, :] += pull
            if first:
                weights[g, cut, :] += w
            new = [half(v) for v in y] + [half(t[j][k]) for j in range(3) for k in range(3)]
            sums = new if sums is None else [s + v for s, v in zip(sums, new)]
            if first:
                wx = [w * x[k] for k in range(3)]
                new = [half(w)] + [half(v) for v in wx]
                new += [half(wx[i] * x[j]) for i, j in SYM]
                consts = new if consts is None else [s + v for s, v in zip(consts, new)]
        put(0, sums, column)
        if first:
            put(16, consts, column)

    def own_view(i, _):
        view(own, meta[1, i], meta[2, i], meta[3, i])
        return 0

    if mode != "far":
        lax.fori_loop(0, own_count, own_view, 0)
    if mode == "own":
        return

    def far_view(i, _):
        at = own_count + i

        @pl.when(meta[0, at] > 0)
        def _():
            view(far, meta[1, at], meta[2, at], meta[3, at])

        return 0

    lax.fori_loop(0, far_count, far_view, 0)

    def finish(g, _):
        sums = None
        for cut in cuts:
            c = [dc[g, j, cut, :] for j in range(3)]
            w = weights[g, cut, :]
            wc = [w * c[j] for j in range(3)]
            twice = 2.0 * (wc[0] * c[0] + wc[1] * c[1] + wc[2] * c[2])
            z_out[g, cut, :] = z_ref[g, cut, :] - (twice - 2.0 * total[g, cut, :]) / (twice + 1.0)
            new = [half(wc[i] * c[j]) for i, j in SYM]
            sums = new if sums is None else [s + v for s, v in zip(sums, new)]
        put(32, sums, rep[g])
        return 0

    lax.fori_loop(0, images, finish, 0)


def pack_kernel(place, maps, conf, own, send, wide):
    _, parts, rows, _, _ = maps.shape
    whole = rows // CHUNK * CHUNK
    left = rows - whole
    tails = [[], []]
    outs = (own, send)
    for k in range(parts + 1):
        both = maps[0, k] if k < parts else conf[0]
        wide[k, 0 : 2 * rows, :] = both.astype(jnp.float32).reshape(2 * rows, LANES)
        for v in range(2):
            body = wide[k, pl.ds(v, whole, stride=2), :].astype(jnp.bfloat16)
            outs[v][0, k * whole : (k + 1) * whole, :] = body
            if left:
                tails[v].append(wide[k, pl.ds(2 * whole + v, left, stride=2), :])
    if left:
        start = (parts + 1) * whole
        spare = tail_rows(rows) - (parts + 1) * left
        for v in range(2):
            lines = tails[v]
            if spare:
                lines = lines + [jnp.zeros((spare, LANES), jnp.float32)]
            outs[v][0, start:, :] = jnp.concatenate(lines, 0).astype(jnp.bfloat16)


def tail_rows(rows):
    return -(-4 * (rows % CHUNK) // CHUNK) * CHUNK


def run_pack(place, slots, maps, conf):
    pairs, parts, rows, _, _ = maps.shape
    high = (parts + 1) * (rows // CHUNK * CHUNK) + tail_rows(rows)
    return pl.pallas_call(
        pack_kernel,
        out_shape=(
            jax.ShapeDtypeStruct((pairs, high, LANES), jnp.bfloat16),
            jax.ShapeDtypeStruct((slots, high, LANES), jnp.bfloat16),
        ),
        grid_spec=pltpu.PrefetchScalarGridSpec(
            num_scalar_prefetch=1,
            grid=(pairs,),
            in_specs=[
                pl.BlockSpec((1, parts, rows, 2, LANES), lambda i, at: (i, 0, 0, 0, 0)),
                pl.BlockSpec((1, rows, 2, LANES), lambda i, at: (i, 0, 0, 0)),
            ],
            out_specs=[
                pl.BlockSpec((1, high, LANES), lambda i, at: (i, 0, 0)),
                pl.BlockSpec((1, high, LANES), lambda i, at: (at[i], 0, 0)),
            ],
            scratch_shapes=[pltpu.VMEM((parts + 1, 2 * rows + 4, LANES), jnp.float32)],
        ),
        compiler_params=pltpu.CompilerParams(vmem_limit_bytes=60 * 1024 * 1024),
    )(place, maps, conf)


def run_step(mode, own_count, meta, rep, coef, z, a, b, *rest):
    images, rows, _ = z.shape
    views = coef.shape[1]
    smem = pl.BlockSpec(memory_space=pltpu.SMEM)
    vmem = pl.BlockSpec(memory_space=pltpu.VMEM)
    field = jax.ShapeDtypeStruct(z.shape, jnp.float32)
    moments = jax.ShapeDtypeStruct((ROWS, views), jnp.float32)
    outs = {"own": (field, field, moments), "far": (field, field, moments), "all": (field, moments)}
    scratch = [pltpu.VMEM((images, 3, rows, LANES), jnp.float32)]
    if mode != "own":
        scratch.append(pltpu.VMEM((images, rows, LANES), jnp.float32))
    return pl.pallas_call(
        functools.partial(step_kernel, mode, own_count),
        out_shape=outs[mode],
        in_specs=[smem] * 3 + [vmem] * (3 + len(rest)),
        out_specs=tuple(vmem for _ in outs[mode]),
        scratch_shapes=scratch,
        compiler_params=pltpu.CompilerParams(vmem_limit_bytes=20 * 1024 * 1024),
        cost_estimate=pl.CostEstimate(
            flops=16 * 1024 * 1024 * 8, bytes_accessed=8 * 1024 * 1024, transcendentals=0
        ),
    )(meta, rep, coef, z, a, b, *rest)


def spread_kernel(size, small, out, send, recv):
    me = lax.axis_index("img")
    barrier = pltpu.get_barrier_semaphore()
    for k in range(1, size):
        peer = lax.rem(me + k, size)
        pl.semaphore_signal(barrier, inc=1, device_id={"img": peer}, device_id_type=MESH)
    pl.semaphore_wait(barrier, size - 1)
    copies = []
    for k in range(1, size):
        peer = lax.rem(me + k, size)
        copy = pltpu.make_async_remote_copy(
            src_ref=small,
            dst_ref=out.at[me],
            send_sem=send.at[k],
            recv_sem=recv.at[me],
            device_id={"img": peer},
            device_id_type=MESH,
        )
        copy.start()
        copies.append(copy)
    out[me] = small[...]
    for k in range(1, size):
        peer = lax.rem(me + k, size)
        pltpu.make_async_remote_copy(
            src_ref=small,
            dst_ref=out.at[peer],
            send_sem=send.at[k],
            recv_sem=recv.at[peer],
            device_id={"img": peer},
            device_id_type=MESH,
        ).wait_recv()
    for copy in copies:
        copy.wait_send()


def run_spread(size, small):
    vmem = pl.BlockSpec(memory_space=pltpu.VMEM)
    return pl.pallas_call(
        functools.partial(spread_kernel, size),
        out_shape=jax.ShapeDtypeStruct((size,) + small.shape, jnp.float32),
        in_specs=[vmem],
        out_specs=vmem,
        scratch_shapes=[pltpu.SemaphoreType.DMA((size,)), pltpu.SemaphoreType.DMA((size,))],
        compiler_params=pltpu.CompilerParams(
            collective_id=1, has_side_effects=True, vmem_limit_bytes=2 * 1024 * 1024
        ),
    )(small)


def share_kernel(
    n_pair, n_img, mom, state, same, state_out, coef_out, buf1, buf2, s1, r1, s2, r2
):
    views = mom.shape[1]
    stages = (("pair", n_pair, buf1, s1, r1), ("img", n_img, buf2, s2, r2))
    barrier = pltpu.get_barrier_semaphore()
    for axis, size, _, _, _ in stages:
        me = lax.axis_index(axis)
        for k in range(1, size):
            peer = lax.rem(me + k, size)
            pl.semaphore_signal(barrier, inc=1, device_id={axis: peer}, device_id_type=MESH)
    pl.semaphore_wait(barrier, n_pair + n_img - 2)

    value = mom[...]
    for axis, size, buf, send, recv in stages:
        me = lax.axis_index(axis)
        buf[me] = value
        copies = []
        for k in range(1, size):
            peer = lax.rem(me + k, size)
            copy = pltpu.make_async_remote_copy(
                src_ref=buf.at[me],
                dst_ref=buf.at[me],
                send_sem=send.at[k],
                recv_sem=recv.at[me],
                device_id={axis: peer},
                device_id_type=MESH,
            )
            copy.start()
            copies.append(copy)
        for k in range(1, size):
            peer = lax.rem(me + k, size)
            pltpu.make_async_remote_copy(
                src_ref=buf.at[peer],
                dst_ref=buf.at[peer],
                send_sem=send.at[k],
                recv_sem=recv.at[peer],
                device_id={axis: peer},
                device_id_type=MESH,
            ).wait_recv()
        value = buf[0]
        for k in range(1, size):
            value = value + buf[k]
        for copy in copies:
            copy.wait_send()

    moments = [value[i : i + 1] for i in range(ROWS)]
    st = [state[i : i + 1, :] for i in range(14)]
    new = update_rows(st, moments, same[...], lambda x: pltpu.roll(x, views // 2, axis=1))
    zero = jnp.zeros_like(new[0])
    state_out[...] = jnp.concatenate(new + [zero] * 2, 0)
    coef_out[...] = jnp.concatenate(coef_rows(new), 0)


def run_share(n_pair, n_img, mom, state, same):
    views = mom.shape[1]
    vmem = pl.BlockSpec(memory_space=pltpu.VMEM)
    return pl.pallas_call(
        functools.partial(share_kernel, n_pair, n_img),
        out_shape=(
            jax.ShapeDtypeStruct((16, views), jnp.float32),
            jax.ShapeDtypeStruct((16, views), jnp.float32),
        ),
        in_specs=[vmem] * 3,
        out_specs=(vmem, vmem),
        scratch_shapes=[
            pltpu.VMEM((n_pair, ROWS, views), jnp.float32),
            pltpu.VMEM((n_img, ROWS, views), jnp.float32),
            pltpu.SemaphoreType.DMA((n_pair,)),
            pltpu.SemaphoreType.DMA((n_pair,)),
            pltpu.SemaphoreType.DMA((n_img,)),
            pltpu.SemaphoreType.DMA((n_img,)),
        ],
        compiler_params=pltpu.CompilerParams(
            collective_id=0, has_side_effects=True, vmem_limit_bytes=8 * 1024 * 1024
        ),
    )(mom, state, same)


def per_device(pair_images, pointmaps, confidence, log_depth, image_params, pair_params):
    pair_dev = pair_images.shape[0]
    img_dev, pix_dev = log_depth.shape
    blocks = lax.axis_size("img")
    n_pair = lax.axis_size("pair")
    slots = max(2, 2 * pair_dev // blocks)
    here = lax.axis_index("img")
    rows = pix_dev // LANES

    pixel = lax.axis_index("pair") * pix_dev + jnp.arange(rows * LANES)
    coord_a = ((pixel % SIDE).astype(jnp.float32) - (SIDE - 1) / 2.0) / SIDE
    coord_b = ((pixel // SIDE).astype(jnp.float32) - (SIDE - 1) / 2.0) / SIDE
    coord_a = coord_a.reshape(rows, LANES)
    coord_b = coord_b.reshape(rows, LANES)

    target = pair_images[:, 1] // img_dev
    hits = (target[:, None] == jnp.arange(blocks)[None, :]).astype(jnp.int32)
    rank = jnp.sum(jnp.cumsum(hits, 0) * hits, 1) - 1
    place = target * slots + rank
    small = jnp.concatenate(
        [
            pair_images.astype(jnp.float32).reshape(-1),
            pair_params.reshape(-1),
            image_params.reshape(-1),
        ]
    )
    count = small.shape[0]
    tiles = -(-count // (8 * LANES))
    small = jnp.pad(small, (0, tiles * 8 * LANES - count)).reshape(tiles * 8, LANES)

    maps = pointmaps.reshape(pair_dev, 2, 3, rows, LANES).transpose(0, 2, 3, 1, 4)
    conf = confidence.reshape(pair_dev, 2, rows, LANES).transpose(0, 2, 1, 3)
    own, send = run_pack(place.astype(jnp.int32), blocks * slots, maps, conf)
    high = own.shape[1]
    small, send = lax.optimization_barrier((small, send))
    small = run_spread(blocks, small)
    small = small.reshape(blocks, -1)[:, :count]
    send = send.reshape(blocks, slots, high, LANES)
    far = lax.all_to_all(send, "img", split_axis=0, concat_axis=0, tiled=True)
    far = far.reshape(blocks * slots, high, LANES)

    cut1, cut2 = 2 * pair_dev, 9 * pair_dev
    all_ids = small[:, :cut1].astype(jnp.int32).reshape(blocks * pair_dev, 2)
    all_pairs = small[:, cut1:cut2].reshape(blocks * pair_dev, 7)
    all_images = small[:, cut2:].reshape(blocks * img_dev, 7)
    image_of = all_ids.T.reshape(-1)
    views = image_of.shape[0]
    pairs = views // 2
    same = (image_of[:, None] == image_of[None, :]).astype(jnp.float32)
    hot = (image_of[None, :] == jnp.arange(blocks * img_dev)[:, None]).astype(jnp.float32)
    by_view = jnp.dot(
        all_images.T, hot, precision=lax.Precision.HIGHEST, preferred_element_type=jnp.float32
    )
    state = jnp.concatenate(
        [jnp.tile(all_pairs.T, (1, 2)), by_view, jnp.zeros((2, views), jnp.float32)], 0
    )
    coef = jnp.concatenate(coef_rows([state[i : i + 1] for i in range(14)]), 0)

    far_ids = all_ids[:, 1].reshape(blocks, pair_dev)
    mine = (far_ids // img_dev == here).astype(jnp.int32)
    far_slot = jnp.arange(blocks)[:, None] * slots + jnp.cumsum(mine, 1) - 1
    mine = mine.reshape(-1)
    meta = jnp.stack(
        [
            jnp.concatenate([jnp.ones((pair_dev,), jnp.int32), mine]),
            jnp.concatenate([jnp.arange(pair_dev), jnp.maximum(far_slot.reshape(-1), 0)]),
            jnp.concatenate([pair_images[:, 0] - here * img_dev, far_ids.reshape(-1) % img_dev]),
            jnp.concatenate([here * pair_dev + jnp.arange(pair_dev), pairs + jnp.arange(pairs)]),
        ]
    ).astype(jnp.int32)
    local = image_of[None, :] == here * img_dev + jnp.arange(img_dev)[:, None]
    rep = jnp.max(jnp.where(local, jnp.arange(views)[None, :], -1), 1)
    seen = rep >= 0
    rep = jnp.maximum(rep, 0).astype(jnp.int32)

    z = log_depth.reshape(img_dev, rows, LANES)
    head = (pair_dev, meta, rep)
    tail = (coord_a, coord_b)
    total, weights, mom = run_step("own", *head, coef, z, *tail, own)
    z, weights, mom = run_step("far", *head, coef, z, *tail, far, total, weights, mom)
    state, coef = run_share(n_pair, blocks, mom, state, same)
    for step in range(1, STEPS):
        z, mom = run_step("all", *head, coef, z, *tail, own, far, weights, mom)
        state, coef = run_share(n_pair, blocks, mom, state, same)

    new_depth = z.reshape(img_dev, pix_dev)
    new_pairs = lax.dynamic_slice(state, (0, here * pair_dev), (7, pair_dev)).T
    new_images = jnp.where(seen[:, None], state[7:14][:, rep].T, image_params)
    return (new_depth, new_images, new_pairs)


def solution(mesh):
    in_specs = (
        P(("groups", "img"), None),
        P(("groups", "img"), None, None, "pair"),
        P(("groups", "img"), None, "pair"),
        P(("groups", "img"), "pair"),
        P(("groups", "img"), None),
        P(("groups", "img"), None),
    )
    out_specs = (
        P(("groups", "img"), "pair"),
        P(("groups", "img"), None),
        P(("groups", "img"), None),
    )
    return jax.shard_map(
        per_device, mesh=mesh, in_specs=in_specs, out_specs=out_specs, check_vma=False
    )
```

```python
import functools

import jax
import jax.numpy as jnp
from jax import lax
from jax.experimental import pallas as pl
from jax.experimental.pallas import tpu as pltpu
from jax.sharding import PartitionSpec as P

SIDE = 224
STEPS = 3
LANES = 128
CHUNK = 16
MESH = pl.DeviceIdType.MESH
ROWS = 40
SYM = ((0, 0), (0, 1), (0, 2), (1, 1), (1, 2), (2, 2))


def rot_rows(w):
    norm = w[0] * w[0] + w[1] * w[1] + w[2] * w[2]
    k = 2.0 / (1.0 + norm)
    cross = [[None, -w[2], w[1]], [w[2], None, -w[0]], [-w[1], w[0], None]]
    out = []
    for i in range(3):
        line = []
        for j in range(3):
            if i == j:
                line.append(1.0 + k * (w[i] * w[i] - norm))
            else:
                line.append(k * (cross[i][j] + w[i] * w[j]))
        out.append(line)
    return out


def rot_grad_rows(w, g):
    norm = w[0] * w[0] + w[1] * w[1] + w[2] * w[2]
    k = 2.0 / (1.0 + norm)
    trace = g[0][0] + g[1][1] + g[2][2]
    skew = [g[2][1] - g[1][2], g[0][2] - g[2][0], g[1][0] - g[0][1]]
    lin = [sum(g[i][j] * w[j] for j in range(3)) for i in range(3)]
    both = [lin[i] + sum(g[j][i] * w[j] for j in range(3)) for i in range(3)]
    value = sum(w[i] * (skew[i] + lin[i]) for i in range(3)) - norm * trace
    return [
        k * (skew[i] + both[i] - 2.0 * w[i] * trace) - k * k * w[i] * value for i in range(3)
    ]


def coef_rows(st):
    factor = jnp.exp(st[0])
    re = rot_rows(st[1:4])
    rg = rot_rows(st[8:11])
    gap = [st[4 + i] - st[11 + i] for i in range(3)]
    rows = []
    for j in range(3):
        for k in range(3):
            rows.append(factor * sum(rg[i][j] * re[i][k] for i in range(3)))
    for j in range(3):
        rows.append(sum(rg[i][j] * gap[i] for i in range(3)))
    rows.append(jnp.exp(-st[7]))
    zero = jnp.zeros_like(rows[0])
    return rows + [zero] * 3


def update_rows(st, mom, same, swap):
    factor = jnp.exp(st[0])
    u, w = st[1:4], st[8:11]
    re, rg = rot_rows(u), rot_rows(w)
    gap = [st[11 + i] - st[4 + i] for i in range(3)]
    d1 = mom[0:3]
    tx = [mom[3 + 3 * j : 6 + 3 * j] for j in range(3)]
    s0 = mom[16]
    s1 = mom[17:20]
    s2, dd = {}, {}
    for n, (i, j) in enumerate(SYM):
        s2[i, j] = s2[j, i] = mom[20 + n]
        dd[i, j] = dd[j, i] = mom[32 + n]
    sre = [[factor * re[i][j] for j in range(3)] for i in range(3)]

    def dot(left, right):
        return left[0] * right[0] + left[1] * right[1] + left[2] * right[2]

    shift = [2.0 * (dot(rg[i], d1) + gap[i] * s0 - dot(sre[i], s1)) for i in range(3)]
    mx = [
        [
            2.0
            * (
                dot(rg[i], [tx[j][k] for j in range(3)])
                + gap[i] * s1[k]
                - dot(sre[i], [s2[j, k] for j in range(3)])
            )
            for k in range(3)
        ]
        for i in range(3)
    ]
    mc = [
        [
            2.0
            * (
                dot(rg[i], [dd[j, k] for j in range(3)])
                + gap[i] * d1[k]
                - dot(sre[i], tx[k])
            )
            for k in range(3)
        ]
        for i in range(3)
    ]
    d_scale = -sum(mx[i][k] * sre[i][k] for i in range(3) for k in range(3))
    d_spin = rot_grad_rows(u, [[-factor * mx[i][k] for k in range(3)] for i in range(3)])
    d_turn = rot_grad_rows(w, mc)
    d_focal = -sum(rg[i][j] * mc[i][j] for i in range(3) for j in range(2))
    grads_p = jnp.concatenate([d_scale] + d_spin + [-x for x in shift] + [s0], 0)
    grads_i = jnp.concatenate([d_focal] + d_turn + shift + [s0], 0)
    grads_p = grads_p + swap(grads_p)
    grads_i = jnp.dot(
        grads_i,
        same,
        precision=lax.Precision.HIGHEST,
        preferred_element_type=jnp.float32,
    )
    rate_p = (0.05, 0.02, 0.02, 0.02, 0.3, 0.3, 0.3)
    rate_i = (0.1, 0.02, 0.02, 0.02, 0.3, 0.3, 0.3)
    down_p = 1.0 / (grads_p[7:8] + 1.0)
    down_i = 1.0 / (grads_i[7:8] + 1.0)
    new = [st[i] - rate_p[i] * grads_p[i : i + 1] * down_p for i in range(7)]
    new += [st[7 + i] - rate_i[i] * grads_i[i : i + 1] * down_i for i in range(7)]
    return new


def step_kernel(mode, own_count, meta, rep, coef, z_ref, a_ref, b_ref, *rest):
    first = mode != "all"
    if mode == "own":
        own, total, weights, mom_out, dc = rest
    elif mode == "far":
        far, total_in, weights_in, before, z_out, weights, mom_out, dc, total = rest
    else:
        own, far, weights, before, z_out, mom_out, dc, total = rest
    images, rows, _ = z_ref.shape
    views = coef.shape[1]
    far_count = meta.shape[1] - own_count
    lane = lax.broadcasted_iota(jnp.int32, (1, views), 1)
    whole = rows // CHUNK * CHUNK
    left = rows - whole
    cuts = [pl.ds(c * CHUNK, CHUNK) for c in range(rows // CHUNK)]
    if left:
        cuts.append(pl.ds(whole, left))

    if mode == "far":
        mom_out[...] = before[...]
        total[...] = total_in[...]
        weights[...] = weights_in[...]
    else:
        mom_out[...] = jnp.zeros_like(mom_out)
        total[...] = jnp.zeros_like(total)
        if mode == "own":
            weights[...] = jnp.zeros_like(weights)
        else:
            mom_out[16:32, :] = before[16:32, :]

    def half(x):
        if x.shape[0] == 16:
            return x[0:8] + x[8:16]
        if x.shape[0] > 8:
            more = jnp.zeros((16 - x.shape[0], LANES), jnp.float32)
            return x[0:8] + jnp.concatenate([x[8:], more], 0)
        if x.shape[0] == 8:
            return x
        return jnp.concatenate([x, jnp.zeros((8 - x.shape[0], LANES), jnp.float32)], 0)

    def fields(data, slot, cut):
        if cut.size == CHUNK:
            return [
                data[slot, pl.ds(k * whole + cut.start, CHUNK), :].astype(jnp.float32)
                for k in range(4)
            ]
        tail = data[slot, 4 * whole :, :].astype(jnp.float32)
        return [tail[k * left : (k + 1) * left] for k in range(4)]

    def put(row, sums, column):
        lines = [jnp.sum(x, 0, keepdims=True) for x in sums]
        count = -(-len(lines) // 8) * 8
        lines += [jnp.zeros_like(lines[0])] * (count - len(lines))
        value = jnp.sum(jnp.concatenate(lines, 0), 1, keepdims=True)
        mom_out[row : row + count, :] += jnp.where(lane == column, value, 0.0)

    def prepare(g, _):
        inv = coef[12, rep[g]]
        for cut in cuts:
            d = jnp.exp(z_ref[g, cut, :])
            near = d * inv
            dc[g, 0, cut, :] = near * a_ref[cut, :]
            dc[g, 1, cut, :] = near * b_ref[cut, :]
            dc[g, 2, cut, :] = d
        return 0

    lax.fori_loop(0, images, prepare, 0)

    def view(data, slot, g, column):
        q = [[coef[3 * j + k, column] for k in range(3)] for j in range(3)]
        p = [coef[9 + j, column] for j in range(3)]
        sums = None
        consts = None
        for cut in cuts:
            *x, w = fields(data, slot, cut)
            y = [dc[g, j, cut, :] * w for j in range(3)]
            t = [[y[j] * x[k] for k in range(3)] for j in range(3)]
            pull = p[0] * y[0] + p[1] * y[1] + p[2] * y[2]
            for j in range(3):
                for k in range(3):
                    pull = pull + q[j][k] * t[j][k]
            total[g, cut, :] += pull
            if first:
                weights[g, cut, :] += w
            new = [half(v) for v in y] + [half(t[j][k]) for j in range(3) for k in range(3)]
            sums = new if sums is None else [s + v for s, v in zip(sums, new)]
            if first:
                wx = [w * x[k] for k in range(3)]
                new = [half(w)] + [half(v) for v in wx]
                new += [half(wx[i] * x[j]) for i, j in SYM]
                consts = new if consts is None else [s + v for s, v in zip(consts, new)]
        put(0, sums, column)
        if first:
            put(16, consts, column)

    def own_view(i, _):
        view(own, meta[1, i], meta[2, i], meta[3, i])
        return 0

    if mode != "far":
        lax.fori_loop(0, own_count, own_view, 0, unroll=2)
    if mode == "own":
        return

    def far_view(i, _):
        at = own_count + i

        @pl.when(meta[0, at] > 0)
        def _():
            view(far, meta[1, at], meta[2, at], meta[3, at])

        return 0

    lax.fori_loop(0, far_count, far_view, 0)

    def finish(g, _):
        sums = None
        for cut in cuts:
            c = [dc[g, j, cut, :] for j in range(3)]
            w = weights[g, cut, :]
            wc = [w * c[j] for j in range(3)]
            twice = 2.0 * (wc[0] * c[0] + wc[1] * c[1] + wc[2] * c[2])
            z_out[g, cut, :] = z_ref[g, cut, :] - (twice - 2.0 * total[g, cut, :]) / (twice + 1.0)
            new = [half(wc[i] * c[j]) for i, j in SYM]
            sums = new if sums is None else [s + v for s, v in zip(sums, new)]
        put(32, sums, rep[g])
        return 0

    lax.fori_loop(0, images, finish, 0)


def pack_kernel(place, maps, conf, own, send, wide):
    pairs, parts, rows, _, _ = maps.shape
    whole = rows // CHUNK * CHUNK
    left = rows - whole

    def pair(i, _):
        tails = [[], []]
        for k in range(parts + 1):
            both = maps[i, k] if k < parts else conf[i]
            wide[k, 0 : 2 * rows, :] = both.astype(jnp.float32).reshape(2 * rows, LANES)
            for v in range(2):
                body = wide[k, pl.ds(v, whole, stride=2), :].astype(jnp.bfloat16)
                if v == 0:
                    own[i, k * whole : (k + 1) * whole, :] = body
                else:
                    send[place[i], k * whole : (k + 1) * whole, :] = body
                if left:
                    tails[v].append(wide[k, pl.ds(2 * whole + v, left, stride=2), :])
        if left:
            start = (parts + 1) * whole
            spare = tail_rows(rows) - (parts + 1) * left
            for v in range(2):
                lines = tails[v]
                if spare:
                    lines = lines + [jnp.zeros((spare, LANES), jnp.float32)]
                tail = jnp.concatenate(lines, 0).astype(jnp.bfloat16)
                if v == 0:
                    own[i, start:, :] = tail
                else:
                    send[place[i], start:, :] = tail
        return 0

    lax.fori_loop(0, pairs, pair, 0)


def tail_rows(rows):
    return -(-4 * (rows % CHUNK) // CHUNK) * CHUNK


def run_pack(place, slots, maps, conf):
    pairs, parts, rows, _, _ = maps.shape
    high = (parts + 1) * (rows // CHUNK * CHUNK) + tail_rows(rows)
    smem = pl.BlockSpec(memory_space=pltpu.SMEM)
    vmem = pl.BlockSpec(memory_space=pltpu.VMEM)
    return pl.pallas_call(
        pack_kernel,
        out_shape=(
            jax.ShapeDtypeStruct((pairs, high, LANES), jnp.bfloat16),
            jax.ShapeDtypeStruct((slots, high, LANES), jnp.bfloat16),
        ),
        in_specs=[smem, vmem, vmem],
        out_specs=(vmem, vmem),
        scratch_shapes=[pltpu.VMEM((parts + 1, 2 * rows + 4, LANES), jnp.float32)],
        compiler_params=pltpu.CompilerParams(vmem_limit_bytes=20 * 1024 * 1024),
    )(place, maps, conf)


def run_step(mode, own_count, meta, rep, coef, z, a, b, *rest):
    images, rows, _ = z.shape
    views = coef.shape[1]
    smem = pl.BlockSpec(memory_space=pltpu.SMEM)
    vmem = pl.BlockSpec(memory_space=pltpu.VMEM)
    field = jax.ShapeDtypeStruct(z.shape, jnp.float32)
    moments = jax.ShapeDtypeStruct((ROWS, views), jnp.float32)
    outs = {"own": (field, field, moments), "far": (field, field, moments), "all": (field, moments)}
    scratch = [pltpu.VMEM((images, 3, rows, LANES), jnp.float32)]
    if mode != "own":
        scratch.append(pltpu.VMEM((images, rows, LANES), jnp.float32))
    return pl.pallas_call(
        functools.partial(step_kernel, mode, own_count),
        out_shape=outs[mode],
        in_specs=[smem] * 3 + [vmem] * (3 + len(rest)),
        out_specs=tuple(vmem for _ in outs[mode]),
        scratch_shapes=scratch,
        compiler_params=pltpu.CompilerParams(vmem_limit_bytes=20 * 1024 * 1024),
        cost_estimate=pl.CostEstimate(
            flops=16 * 1024 * 1024 * 8, bytes_accessed=8 * 1024 * 1024, transcendentals=0
        ),
    )(meta, rep, coef, z, a, b, *rest)


def spread_kernel(size, small, out, send, recv):
    me = lax.axis_index("img")
    barrier = pltpu.get_barrier_semaphore()
    for k in range(1, size):
        peer = lax.rem(me + k, size)
        pl.semaphore_signal(barrier, inc=1, device_id={"img": peer}, device_id_type=MESH)
    pl.semaphore_wait(barrier, size - 1)
    copies = []
    for k in range(1, size):
        peer = lax.rem(me + k, size)
        copy = pltpu.make_async_remote_copy(
            src_ref=small,
            dst_ref=out.at[me],
            send_sem=send.at[k],
            recv_sem=recv.at[me],
            device_id={"img": peer},
            device_id_type=MESH,
        )
        copy.start()
        copies.append(copy)
    out[me] = small[...]
    for k in range(1, size):
        peer = lax.rem(me + k, size)
        pltpu.make_async_remote_copy(
            src_ref=small,
            dst_ref=out.at[peer],
            send_sem=send.at[k],
            recv_sem=recv.at[peer],
            device_id={"img": peer},
            device_id_type=MESH,
        ).wait_recv()
    for copy in copies:
        copy.wait_send()


def run_spread(size, small):
    vmem = pl.BlockSpec(memory_space=pltpu.VMEM)
    return pl.pallas_call(
        functools.partial(spread_kernel, size),
        out_shape=jax.ShapeDtypeStruct((size,) + small.shape, jnp.float32),
        in_specs=[vmem],
        out_specs=vmem,
        scratch_shapes=[pltpu.SemaphoreType.DMA((size,)), pltpu.SemaphoreType.DMA((size,))],
        compiler_params=pltpu.CompilerParams(
            collective_id=1, has_side_effects=True, vmem_limit_bytes=2 * 1024 * 1024
        ),
    )(small)


def share_kernel(
    n_pair, n_img, mom, state, same, state_out, coef_out, buf1, buf2, s1, r1, s2, r2
):
    views = mom.shape[1]
    stages = (("pair", n_pair, buf1, s1, r1), ("img", n_img, buf2, s2, r2))
    barrier = pltpu.get_barrier_semaphore()
    for axis, size, _, _, _ in stages:
        me = lax.axis_index(axis)
        for k in range(1, size):
            peer = lax.rem(me + k, size)
            pl.semaphore_signal(barrier, inc=1, device_id={axis: peer}, device_id_type=MESH)
    pl.semaphore_wait(barrier, n_pair + n_img - 2)

    value = mom[...]
    for axis, size, buf, send, recv in stages:
        me = lax.axis_index(axis)
        buf[me] = value
        copies = []
        for k in range(1, size):
            peer = lax.rem(me + k, size)
            copy = pltpu.make_async_remote_copy(
                src_ref=buf.at[me],
                dst_ref=buf.at[me],
                send_sem=send.at[k],
                recv_sem=recv.at[me],
                device_id={axis: peer},
                device_id_type=MESH,
            )
            copy.start()
            copies.append(copy)
        for k in range(1, size):
            peer = lax.rem(me + k, size)
            pltpu.make_async_remote_copy(
                src_ref=buf.at[peer],
                dst_ref=buf.at[peer],
                send_sem=send.at[k],
                recv_sem=recv.at[peer],
                device_id={axis: peer},
                device_id_type=MESH,
            ).wait_recv()
        value = buf[0]
        for k in range(1, size):
            value = value + buf[k]
        for copy in copies:
            copy.wait_send()

    moments = [value[i : i + 1] for i in range(ROWS)]
    st = [state[i : i + 1, :] for i in range(14)]
    new = update_rows(st, moments, same[...], lambda x: pltpu.roll(x, views // 2, axis=1))
    zero = jnp.zeros_like(new[0])
    state_out[...] = jnp.concatenate(new + [zero] * 2, 0)
    coef_out[...] = jnp.concatenate(coef_rows(new), 0)


def run_share(n_pair, n_img, mom, state, same):
    views = mom.shape[1]
    vmem = pl.BlockSpec(memory_space=pltpu.VMEM)
    return pl.pallas_call(
        functools.partial(share_kernel, n_pair, n_img),
        out_shape=(
            jax.ShapeDtypeStruct((16, views), jnp.float32),
            jax.ShapeDtypeStruct((16, views), jnp.float32),
        ),
        in_specs=[vmem] * 3,
        out_specs=(vmem, vmem),
        scratch_shapes=[
            pltpu.VMEM((n_pair, ROWS, views), jnp.float32),
            pltpu.VMEM((n_img, ROWS, views), jnp.float32),
            pltpu.SemaphoreType.DMA((n_pair,)),
            pltpu.SemaphoreType.DMA((n_pair,)),
            pltpu.SemaphoreType.DMA((n_img,)),
            pltpu.SemaphoreType.DMA((n_img,)),
        ],
        compiler_params=pltpu.CompilerParams(
            collective_id=0, has_side_effects=True, vmem_limit_bytes=8 * 1024 * 1024
        ),
    )(mom, state, same)


def per_device(pair_images, pointmaps, confidence, log_depth, image_params, pair_params):
    pair_dev = pair_images.shape[0]
    img_dev, pix_dev = log_depth.shape
    blocks = lax.axis_size("img")
    n_pair = lax.axis_size("pair")
    slots = max(2, 2 * pair_dev // blocks)
    here = lax.axis_index("img")
    rows = pix_dev // LANES

    pixel = lax.axis_index("pair") * pix_dev + jnp.arange(rows * LANES)
    coord_a = ((pixel % SIDE).astype(jnp.float32) - (SIDE - 1) / 2.0) / SIDE
    coord_b = ((pixel // SIDE).astype(jnp.float32) - (SIDE - 1) / 2.0) / SIDE
    coord_a = coord_a.reshape(rows, LANES)
    coord_b = coord_b.reshape(rows, LANES)

    target = pair_images[:, 1] // img_dev
    hits = (target[:, None] == jnp.arange(blocks)[None, :]).astype(jnp.int32)
    rank = jnp.sum(jnp.cumsum(hits, 0) * hits, 1) - 1
    place = target * slots + rank
    ids = jnp.pad(pair_images.astype(jnp.float32), ((0, img_dev), (0, LANES - 2)))
    poses = jnp.pad(pair_params, ((0, img_dev), (2, LANES - 9)))
    cameras = jnp.pad(image_params, ((pair_dev, 0), (2, LANES - 9)))
    small = ids + poses + cameras
    small = run_spread(blocks, small)

    maps = pointmaps.reshape(pair_dev, 2, 3, rows, LANES).transpose(0, 2, 3, 1, 4)
    conf = confidence.reshape(pair_dev, 2, rows, LANES).transpose(0, 2, 1, 3)
    own, send = run_pack(place.astype(jnp.int32), blocks * slots, maps, conf)
    high = own.shape[1]
    small, send = lax.optimization_barrier((small, send))
    send = send.reshape(blocks, slots, high, LANES)
    far = lax.all_to_all(send, "img", split_axis=0, concat_axis=0, tiled=True)
    far = far.reshape(blocks * slots, high, LANES)

    all_ids = small[:, :pair_dev, :2].astype(jnp.int32).reshape(blocks * pair_dev, 2)
    all_pairs = small[:, :pair_dev, 2:9].reshape(blocks * pair_dev, 7)
    all_images = small[:, pair_dev:, 2:9].reshape(blocks * img_dev, 7)
    image_of = all_ids.T.reshape(-1)
    views = image_of.shape[0]
    pairs = views // 2
    same = (image_of[:, None] == image_of[None, :]).astype(jnp.float32)
    hot = (image_of[None, :] == jnp.arange(blocks * img_dev)[:, None]).astype(jnp.float32)
    by_view = jnp.dot(
        all_images.T, hot, precision=lax.Precision.HIGHEST, preferred_element_type=jnp.float32
    )
    state = jnp.concatenate(
        [jnp.tile(all_pairs.T, (1, 2)), by_view, jnp.zeros((2, views), jnp.float32)], 0
    )
    coef = jnp.concatenate(coef_rows([state[i : i + 1] for i in range(14)]), 0)

    far_ids = all_ids[:, 1].reshape(blocks, pair_dev)
    mine = (far_ids // img_dev == here).astype(jnp.int32)
    far_slot = jnp.arange(blocks)[:, None] * slots + jnp.cumsum(mine, 1) - 1
    mine = mine.reshape(-1)
    meta = jnp.stack(
        [
            jnp.concatenate([jnp.ones((pair_dev,), jnp.int32), mine]),
            jnp.concatenate([jnp.arange(pair_dev), jnp.maximum(far_slot.reshape(-1), 0)]),
            jnp.concatenate([pair_images[:, 0] - here * img_dev, far_ids.reshape(-1) % img_dev]),
            jnp.concatenate([here * pair_dev + jnp.arange(pair_dev), pairs + jnp.arange(pairs)]),
        ]
    ).astype(jnp.int32)
    local = image_of[None, :] == here * img_dev + jnp.arange(img_dev)[:, None]
    rep = jnp.max(jnp.where(local, jnp.arange(views)[None, :], -1), 1)
    seen = rep >= 0
    rep = jnp.maximum(rep, 0).astype(jnp.int32)

    z = log_depth.reshape(img_dev, rows, LANES)
    head = (pair_dev, meta, rep)
    tail = (coord_a, coord_b)
    total, weights, mom = run_step("own", *head, coef, z, *tail, own)
    z, weights, mom = run_step("far", *head, coef, z, *tail, far, total, weights, mom)
    state, coef = run_share(n_pair, blocks, mom, state, same)
    for step in range(1, STEPS):
        z, mom = run_step("all", *head, coef, z, *tail, own, far, weights, mom)
        state, coef = run_share(n_pair, blocks, mom, state, same)

    new_depth = z.reshape(img_dev, pix_dev)
    new_pairs = lax.dynamic_slice(state, (0, here * pair_dev), (7, pair_dev)).T
    new_images = jnp.where(seen[:, None], state[7:14][:, rep].T, image_params)
    return (new_depth, new_images, new_pairs)


def solution(mesh):
    in_specs = (
        P(("groups", "img"), None),
        P(("groups", "img"), None, None, "pair"),
        P(("groups", "img"), None, "pair"),
        P(("groups", "img"), "pair"),
        P(("groups", "img"), None),
        P(("groups", "img"), None),
    )
    out_specs = (
        P(("groups", "img"), "pair"),
        P(("groups", "img"), None),
        P(("groups", "img"), None),
    )
    return jax.shard_map(
        per_device, mesh=mesh, in_specs=in_specs, out_specs=out_specs, check_vma=False
    )
```
